32 devices in a mesh: sector: 8 (over z, y), dof: 4 (over x, core).
Axes of the slice: x: 2, y: 2, z: 4, core: 2. Of those that a mesh axis runs over, the one named last changes fastest.
Arguments:
- load_history: bfloat16 [8, 64, 6144], P('sector', None, 'dof'), may hold values from -6 to 6
- sector_basis: bfloat16 [6144, 1536], P('dof'), may hold values from -0.078125 to 0.078125
- harmonic_modes: bfloat16 [8, 1536, 256], P('sector'), may hold values from -0.15625 to 0.15625
- stress_basis: bfloat16 [1536, 6144], P(None, 'dof'), may hold values from -0.375 to 0.375
- mode_decay: float32 [8, 256], P('sector'), may hold values from 0.01 to 0.3
- mode_phase: float32 [8, 256], P('sector'), may hold values from 0.05 to 1.5
- mode_count: int32 [8], P('sector'), may hold values from 64 to 256, as said below
- slot_harmonic: int32 [8], replicated, may hold values from 0 to 7, each once
Outputs:
- stress_field: bfloat16 [8, 64, 6144], P('sector', None, 'dof')
The draws below stay inside these ranges and needn't reach their ends.
Inputs may be any that keep to these rules, and one draw needn't show every extreme that they name: Slot modes from mode_count on are left out; some slot has 256 live modes and some 256 // 4. `slot_harmonic`: every harmonic component is held by exactly one slot.
All inputs are finite; a program needn't handle non-finite values.
Results may differ from the reference program's by a relative error of at most 0.025.
Values may be sent and summed in bfloat16 or wider, within the bound.
A program may use at most 64 MiB of HBM per device.

```python
import math
import jax
import jax.numpy as jnp
from jax import lax

STEPS = 64
REDUCED = 1536
MODES = 256
SECTORS = 8
DOFS = 6144
STRESS = 6144


def draw_mode_count(key, part):
    key_values, key_top, key_low = jax.random.split(key, 3)
    counts = jax.random.randint(key_values, (SECTORS,), MODES // 4, MODES + 1, dtype=jnp.int32)
    top_slot = jax.random.randint(key_top, (), 0, SECTORS, dtype=jnp.int32)
    step_away = jax.random.randint(key_low, (), 1, SECTORS, dtype=jnp.int32)
    low_slot = (top_slot + step_away) % SECTORS
    counts = counts.at[top_slot].set(MODES)
    counts = counts.at[low_slot].set(MODES // 4)
    return counts


def steps_of(own_key, extent, shards, smallest, largest):
    factor_of, own = 1.0, jax.random.fold_in(own_key, 6)
    for dim, parts in shards:
        heights = jnp.exp(jax.random.uniform(jax.random.fold_in(own, dim), (parts,), jnp.float32, smallest / len(shards), largest / len(shards)))
        factor_of = factor_of * jnp.repeat(heights, extent[dim] // parts).reshape([-1 if axis == dim else 1 for axis in range(len(extent))])
    return factor_of


def gaussian(rng, extent, deviation, most, cuts=(), held_as=jnp.bfloat16):
    values = jax.random.normal(rng, extent, jnp.float32) * deviation
    if len(cuts) > 0:
        values = steps_of(rng, extent, cuts, -0.22, 0.18) * values
    return jnp.clip(values, min=-most, max=most).astype(held_as)


def setup_inputs(seed: int = 0) -> dict:
    streams_of = jax.random.split(jax.random.key(seed), 9)
    load_history = gaussian(streams_of[0], (SECTORS, STEPS, DOFS), 1.0, 6.0, ((0, 8), (2, 4)))
    sector_basis = gaussian(streams_of[1], (DOFS, REDUCED), DOFS ** -0.5, 0.078125, ((0, 4),))
    harmonic_modes = gaussian(streams_of[2], (SECTORS, REDUCED, MODES), REDUCED ** -0.5, 0.15625, ((0, 8),))
    stress_basis = gaussian(streams_of[3], (REDUCED, STRESS), MODES ** -0.5, 0.375, ((1, 4),))
    mode_decay = jnp.clip(jnp.exp(math.log(0.3) - 3.4011974 * jax.random.uniform(streams_of[4], (SECTORS, MODES), jnp.float32) ** steps_of(streams_of[4], (SECTORS, MODES), ((0, 8),), -0.2, 0.2)), 0.01, 0.3)
    mode_phase = jnp.clip(0.05 + 1.45 * jax.random.uniform(streams_of[5], (SECTORS, MODES), jnp.float32) ** steps_of(streams_of[5], (SECTORS, MODES), ((0, 8),), -0.2, 0.2), 0.05, 1.5)
    mode_count = draw_mode_count(jax.random.fold_in(streams_of[8], 71), 0)
    slot_harmonic = jax.random.permutation(streams_of[7], SECTORS).astype(jnp.int32)
    return dict(load_history=load_history, sector_basis=sector_basis, harmonic_modes=harmonic_modes, stress_basis=stress_basis, mode_decay=mode_decay, mode_phase=mode_phase, mode_count=mode_count, slot_harmonic=slot_harmonic)


def transform_table(slot_harmonic):
    count_all = slot_harmonic.shape[0]
    half_count = count_all // 2
    sine_rows = slot_harmonic > half_count
    harmonic_order = jnp.where(sine_rows, slot_harmonic - half_count, slot_harmonic).astype(jnp.int32)
    sector_index = jnp.arange(count_all, dtype=jnp.int32)
    residue = harmonic_order[:, None] * sector_index[None, :] % count_all
    phase_angle = residue.astype(jnp.float32) * jnp.float32(2.0 * math.pi / count_all)
    wave_table = jnp.where(sine_rows[:, None], jnp.sin(phase_angle), jnp.cos(phase_angle))
    single = (slot_harmonic == 0) | (slot_harmonic == half_count)
    weight = jnp.where(single, jnp.float32(1.0 / count_all), jnp.float32(2.0 / count_all))
    return jnp.sqrt(weight)[:, None] * wave_table

def filter_kernel(decay_rates, phase_steps, steps_count):
    time_index = jnp.arange(steps_count, dtype=jnp.int32)
    offset = time_index[:, None] - time_index[None, :]
    causal = offset >= 0
    lag_value = jnp.maximum(offset, 0).astype(jnp.float32)
    gain_factor = jnp.sqrt(1.0 - jnp.exp(-2.0 * decay_rates))
    shape_table = gain_factor[..., None, None] * jnp.exp(-decay_rates[..., None, None] * lag_value) * jnp.cos(phase_steps[..., None, None] * lag_value)
    return jnp.where(causal, shape_table, jnp.float32(0.0))

def reference(load_history, sector_basis, harmonic_modes, stress_basis, mode_decay, mode_phase, mode_count, slot_harmonic):
    highest = lax.Precision.HIGHEST
    table = transform_table(slot_harmonic)
    count_all, steps_count, rows_all = load_history.shape
    flat_loads = load_history.reshape(count_all * steps_count, rows_all).astype(jnp.float32)
    reduced = jnp.dot(flat_loads, sector_basis.astype(jnp.float32), precision=highest)
    reduced = lax.optimization_barrier(reduced.astype(jnp.bfloat16)).reshape(count_all, steps_count, -1)
    spectrum = jnp.einsum('ks,stc->ktc', table, reduced.astype(jnp.float32), precision=highest)
    spectrum = lax.optimization_barrier(spectrum.astype(jnp.bfloat16))
    modes_wide = harmonic_modes.astype(jnp.float32)
    modal = jnp.einsum('ktc,kcm->ktm', spectrum.astype(jnp.float32), modes_wide, precision=highest)
    live = jnp.arange(harmonic_modes.shape[2], dtype=jnp.int32)[None, :] < mode_count[:, None]
    modal = modal * live[:, None, :].astype(jnp.float32)
    kernel = filter_kernel(mode_decay, mode_phase, steps_count)
    response = jnp.einsum('kmtu,kum->ktm', kernel, modal, precision=highest)
    response = lax.optimization_barrier(response.astype(jnp.bfloat16))
    returned = jnp.einsum('ktm,kcm->ktc', response.astype(jnp.float32), modes_wide, precision=highest)
    returned = lax.optimization_barrier(returned.astype(jnp.bfloat16))
    back = jnp.einsum('ks,ktc->stc', table, returned.astype(jnp.float32), precision=highest)
    back = lax.optimization_barrier(back.astype(jnp.bfloat16))
    flat_back = back.reshape(count_all * steps_count, -1).astype(jnp.float32)
    stress_field = jnp.dot(flat_back, stress_basis.astype(jnp.float32), precision=highest)
    return stress_field.astype(jnp.bfloat16).reshape(count_all, steps_count, -1)
```

```python
import functools
import math

import jax
import jax.numpy as jnp
from jax import lax
from jax.experimental import pallas as pl
from jax.experimental.pallas import tpu as pltpu
from jax.sharding import PartitionSpec as P

MESH = pl.DeviceIdType.MESH
ROWS = 16
HALVES = 2


def each(count, body):
    if count <= 32:
        for index in range(count):
            body(index)
    else:

        @pl.loop(0, count)
        def _(index):
            body(index)


def kernel(
    sectors,
    dofs,
    load_hbm,
    basis_hbm,
    modes_hbm,
    stress_hbm,
    decay_ref,
    phase_ref,
    count_ref,
    slot_ref,
    out_ref,
    load_v,
    basis_v,
    modes_v,
    stress_v,
    part_send,
    part_recv,
    spec_send,
    spec_recv,
    ret_send,
    ret_recv,
    back_send,
    back_recv,
    fwd_table,
    bwd_table,
    lag_table,
    padded,
    local_sem,
    basis_sem,
    send_sem,
    part_sem,
    spec_sem,
    ret_sem,
    back_sem,
):
    steps, reduced = load_v.shape
    width = reduced // dofs
    half = reduced // HALVES
    groups = steps // ROWS
    per_half = dofs // HALVES
    mixers = groups * dofs
    devices = sectors * dofs
    stride = devices // mixers
    f32, bf16 = jnp.float32, jnp.bfloat16

    own_sector = lax.axis_index("sector")
    own_dof = lax.axis_index("dof")
    me = own_sector * dofs + own_dof
    is_mixer = lax.rem(me, stride) == 0
    own_piece = me // stride
    own_group = own_piece // dofs
    own_rest = lax.rem(own_piece, dofs)
    own_part = lax.rem(own_rest, HALVES) * per_half + own_rest // HALVES

    def device(index):
        return (index // dofs, lax.rem(index, dofs))

    def mixer_of(group, part):
        return (group * dofs + lax.rem(part, per_half) * HALVES + part // per_half) * stride

    load_copy = pltpu.make_async_copy(load_hbm.at[0], load_v, local_sem.at[0])
    load_copy.start()
    basis_copies = []
    for turn in range(HALVES):
        which = lax.rem(own_sector + own_dof + turn, HALVES)
        columns = pl.ds(pl.multiple_of(which * half, 128), half)
        copy = pltpu.make_async_copy(
            basis_hbm.at[:, columns], basis_v.at[turn], basis_sem.at[turn]
        )
        copy.start()
        basis_copies.append(copy)
    modes_copy = pltpu.make_async_copy(modes_hbm.at[0], modes_v, local_sem.at[1])
    modes_copy.start()
    stress_copy = pltpu.make_async_copy(stress_hbm, stress_v, local_sem.at[2])
    stress_copy.start()

    barrier = pltpu.get_barrier_semaphore()

    def greet_mixer(index):
        target = index * stride

        @pl.when(target != me)
        def _():
            pl.semaphore_signal(barrier, inc=1, device_id=device(target), device_id_type=MESH)

    each(mixers, greet_mixer)

    @pl.when(is_mixer)
    def _():
        def greet_other(index):
            target = index // (stride - 1) * stride + 1 + index % (stride - 1)
            pl.semaphore_signal(barrier, inc=1, device_id=device(target), device_id_type=MESH)

        each(devices - mixers, greet_other)

    def send_to(src, dst, sem, out_sem, target):
        @pl.when(target != me)
        def _():
            pltpu.make_async_remote_copy(
                src_ref=src,
                dst_ref=dst,
                send_sem=out_sem,
                recv_sem=sem,
                device_id=device(target),
                device_id_type=MESH,
            ).start()

        @pl.when(target == me)
        def _():
            pltpu.make_async_copy(src, dst, sem).start()

    load_copy.wait()
    for turn in range(HALVES):
        which = lax.rem(own_sector + own_dof + turn, HALVES)
        basis_copies[turn].wait()
        product = jnp.dot(load_v[...], basis_v[turn], preferred_element_type=f32).astype(bf16)
        for inner in range(per_half):
            part_send[turn, inner] = product[:, inner * width : (inner + 1) * width].reshape(
                groups, ROWS, width
            )
        if turn == 0:

            @pl.when(is_mixer)
            def _():
                pl.semaphore_wait(barrier, devices - 1)

            @pl.when(jnp.logical_not(is_mixer))
            def _():
                pl.semaphore_wait(barrier, mixers)

        for inner in range(per_half):
            part = which * per_half + inner
            for group in range(groups):
                send_to(
                    part_send.at[turn, inner, group],
                    part_recv.at[own_sector, own_dof],
                    part_sem,
                    send_sem.at[0],
                    mixer_of(group, part),
                )

    decay = decay_ref[...]
    lag = lax.broadcasted_iota(jnp.int32, lag_table.shape, 0).astype(f32)
    gain = jnp.sqrt(1.0 - jnp.exp(-2.0 * decay))
    lag_table[...] = gain * jnp.exp(-decay * lag) * jnp.cos(phase_ref[...] * lag)
    padded[pl.ds(0, steps), :] = jnp.zeros((steps, padded.shape[1]), f32)

    @pl.when(is_mixer)
    def _():
        wide = sectors * ROWS
        row = lax.broadcasted_iota(jnp.int32, (sectors, wide), 0)
        sector = (lax.broadcasted_iota(jnp.int32, (sectors, wide), 1) // ROWS).astype(f32)
        harmonic = jnp.zeros((sectors, wide), f32)
        for slot in range(sectors):
            harmonic = jnp.where(row == slot, slot_ref[slot].astype(f32), harmonic)
        middle = float(sectors // 2)
        sine = harmonic > middle
        order = jnp.where(sine, harmonic - middle, harmonic)
        turns = order * sector
        residue = turns - float(sectors) * jnp.floor(turns * (1.0 / sectors))
        angle = residue * jnp.float32(2.0 * math.pi / sectors)
        wave = jnp.cos(angle - jnp.where(sine, jnp.float32(0.5 * math.pi), jnp.float32(0.0)))
        single = (harmonic == 0.0) | (harmonic == middle)
        weight = jnp.where(single, jnp.float32(math.sqrt(1.0 / sectors)), jnp.float32(math.sqrt(2.0 / sectors)))
        small = weight * wave
        table = jnp.broadcast_to(small[:, None, :], (sectors, ROWS, wide)).reshape(wide, wide)
        left = lax.broadcasted_iota(jnp.int32, (wide, wide), 0) % ROWS
        right = lax.broadcasted_iota(jnp.int32, (wide, wide), 1) % ROWS
        table = jnp.where(left == right, table, 0.0)
        for where_to, values in ((fwd_table, table), (bwd_table, table.T)):
            high = values.astype(bf16)
            where_to[0] = high
            where_to[1] = (values - high.astype(f32)).astype(bf16)

    def mix(table_ref, values):
        return (
            jnp.dot(table_ref[0], values, preferred_element_type=f32)
            + jnp.dot(table_ref[1], values, preferred_element_type=f32)
        ).astype(bf16)

    own_half = own_part // per_half
    own_columns = pl.ds(pl.multiple_of(lax.rem(own_part, per_half) * width, 128), width)

    def spread(source, sink, sem, out_sem):
        dst = sink.at[own_half, own_group, :, own_columns]

        def send(index):
            target = lax.rem(me + index + 1, devices)
            pltpu.make_async_remote_copy(
                src_ref=source.at[target // dofs],
                dst_ref=dst,
                send_sem=out_sem,
                recv_sem=sem.at[own_half],
                device_id=device(target),
                device_id_type=MESH,
            ).start()

        each(devices - 1, send)
        pltpu.make_async_copy(source.at[own_sector], dst, sem.at[own_half]).start()

    @pl.when(is_mixer)
    def _():
        pltpu.make_async_copy(part_recv, part_recv, part_sem).wait()
        total = part_recv[:, 0].astype(f32)
        for dof in range(1, dofs):
            total = total + part_recv[:, dof].astype(f32)
        values = total.reshape(sectors * ROWS, width).astype(bf16)
        spec_send[...] = mix(fwd_table, values).reshape(sectors, ROWS, width)
        spread(spec_send, spec_recv, spec_sem, send_sem.at[1])

    modes_copy.wait()
    modal = jnp.zeros((steps, modes_v.shape[1]), f32)
    for which in range(HALVES):
        pltpu.make_async_copy(
            spec_recv.at[which], spec_recv.at[which], spec_sem.at[which]
        ).wait()
        modal = modal + jnp.dot(
            spec_recv[which].reshape(steps, half),
            modes_v[pl.ds(which * half, half), :],
            preferred_element_type=f32,
        )
    mode = lax.broadcasted_iota(jnp.int32, modal.shape, 1)
    padded[pl.ds(steps, steps), :] = jnp.where(mode < count_ref[0], modal, 0.0)
    cut = steps // 2
    upper = jnp.zeros((cut, modal.shape[1]), f32)
    lower = jnp.zeros((cut, modal.shape[1]), f32)
    for n in range(steps):
        scale = lag_table[pl.ds(n, 1), :]
        if n < cut:
            upper = upper + scale * padded[pl.ds(steps - n, cut), :]
        lower = lower + scale * padded[pl.ds(steps + cut - n, cut), :]
    response = jnp.concatenate([upper, lower], axis=0).astype(bf16)
    own_rows = modes_v[pl.ds(pl.multiple_of(own_dof * width, 128), width), :]
    returned = lax.dot_general(
        response, own_rows, (((1,), (1,)), ((), ())), preferred_element_type=f32
    )
    ret_send[...] = returned.astype(bf16).reshape(groups, ROWS, width)
    for group in range(groups):
        send_to(
            ret_send.at[group],
            ret_recv.at[own_sector],
            ret_sem,
            send_sem.at[2],
            mixer_of(group, own_dof),
        )

    @pl.when(is_mixer)
    def _():
        pltpu.make_async_copy(ret_recv, ret_recv, ret_sem).wait()
        values = ret_recv[...].reshape(sectors * ROWS, width)
        back_send[...] = mix(bwd_table, values).reshape(sectors, ROWS, width)
        spread(back_send, back_recv, back_sem, send_sem.at[3])

    stress_copy.wait()
    field = jnp.zeros((steps, out_ref.shape[2]), f32)
    for which in range(HALVES):
        pltpu.make_async_copy(
            back_recv.at[which], back_recv.at[which], back_sem.at[which]
        ).wait()
        field = field + jnp.dot(
            back_recv[which].reshape(steps, half),
            stress_v[pl.ds(which * half, half), :],
            preferred_element_type=f32,
        )
    out_ref[0] = field.astype(bf16)

    def sent(ref, sem):
        pltpu.make_async_copy(ref, ref, sem).wait()

    @pl.when(is_mixer)
    def _():
        for index in range(dofs):
            ref = part_send.at[index // per_half, index % per_half]
            sent(ref.at[pl.ds(0, groups - (index == 0))], send_sem.at[0])
        for sem in (send_sem.at[1], send_sem.at[3]):
            sent(part_recv.at[pl.ds(0, sectors - 1)], sem)
            sent(part_recv.at[0, pl.ds(0, dofs - 1)], sem)

    @pl.when(jnp.logical_not(is_mixer))
    def _():
        sent(part_send, send_sem.at[0])

    own_return = is_mixer & (own_part == own_dof)

    @pl.when(own_return)
    def _():
        sent(ret_send.at[pl.ds(0, groups - 1)], send_sem.at[2])

    @pl.when(jnp.logical_not(own_return))
    def _():
        sent(ret_send, send_sem.at[2])


def local(
    sectors,
    dofs,
    load_history,
    sector_basis,
    harmonic_modes,
    stress_basis,
    mode_decay,
    mode_phase,
    mode_count,
    slot_harmonic,
):
    _, steps, rows = load_history.shape
    reduced = sector_basis.shape[1]
    modes = harmonic_modes.shape[2]
    stress = stress_basis.shape[1]
    width = reduced // dofs
    groups = steps // ROWS
    half = reduced // HALVES
    wide = sectors * ROWS
    bf16, f32 = jnp.bfloat16, jnp.float32
    flops = 2 * steps * reduced * (rows + stress + 2 * modes)
    return pl.pallas_call(
        functools.partial(kernel, sectors, dofs),
        out_shape=jax.ShapeDtypeStruct((1, steps, stress), bf16),
        in_specs=[pl.BlockSpec(memory_space=pl.ANY)] * 4
        + [pl.BlockSpec(memory_space=pltpu.VMEM)] * 2
        + [pl.BlockSpec(memory_space=pltpu.SMEM)] * 2,
        out_specs=pl.BlockSpec(memory_space=pltpu.VMEM),
        scratch_shapes=[
            pltpu.VMEM((steps, rows), bf16),
            pltpu.VMEM((HALVES, rows, half), bf16),
            pltpu.VMEM((reduced, modes), bf16),
            pltpu.VMEM((reduced, stress), bf16),
            pltpu.VMEM((HALVES, dofs // HALVES, groups, ROWS, width), bf16),
            pltpu.VMEM((sectors, dofs, ROWS, width), bf16),
            pltpu.VMEM((sectors, ROWS, width), bf16),
            pltpu.VMEM((HALVES, groups, ROWS, half), bf16),
            pltpu.VMEM((groups, ROWS, width), bf16),
            pltpu.VMEM((sectors, ROWS, width), bf16),
            pltpu.VMEM((sectors, ROWS, width), bf16),
            pltpu.VMEM((HALVES, groups, ROWS, half), bf16),
            pltpu.VMEM((2, wide, wide), bf16),
            pltpu.VMEM((2, wide, wide), bf16),
            pltpu.VMEM((steps, modes), f32),
            pltpu.VMEM((2 * steps, modes), f32),
            pltpu.SemaphoreType.DMA((3,)),
            pltpu.SemaphoreType.DMA((HALVES,)),
            pltpu.SemaphoreType.DMA((4,)),
            pltpu.SemaphoreType.DMA,
            pltpu.SemaphoreType.DMA((HALVES,)),
            pltpu.SemaphoreType.DMA,
            pltpu.SemaphoreType.DMA((HALVES,)),
        ],
        compiler_params=pltpu.CompilerParams(
            collective_id=0, has_side_effects=True, vmem_limit_bytes=48 * 1024 * 1024
        ),
        cost_estimate=pl.CostEstimate(
            flops=flops, bytes_accessed=2 * reduced * (rows + stress), transcendentals=0
        ),
    )(
        load_history,
        sector_basis,
        harmonic_modes,
        stress_basis,
        mode_decay,
        mode_phase,
        mode_count,
        slot_harmonic,
    )


def solution(mesh):
    return jax.shard_map(
        functools.partial(local, mesh.shape["sector"], mesh.shape["dof"]),
        mesh=mesh,
        in_specs=(
            P("sector", None, "dof"),
            P("dof", None),
            P("sector", None, None),
            P(None, "dof"),
            P("sector", None),
            P("sector", None),
            P("sector"),
            P(),
        ),
        out_specs=P("sector", None, "dof"),
        check_vma=False,
    )
```

```python
import functools
import math

import jax
import jax.numpy as jnp
from jax import lax
from jax.experimental import pallas as pl
from jax.experimental.pallas import tpu as pltpu
from jax.sharding import PartitionSpec as P

MESH = pl.DeviceIdType.MESH
ROWS = 16
HALVES = 2


def each(count, body):
    if count <= 32:
        for index in range(count):
            body(index)
    else:

        @pl.loop(0, count)
        def _(index):
            body(index)


def kernel(
    sectors,
    dofs,
    load_hbm,
    basis_hbm,
    modes_hbm,
    stress_hbm,
    decay_hbm,
    phase_hbm,
    count_hbm,
    slot_hbm,
    out_ref,
    load_v,
    basis_v,
    modes_v,
    stress_v,
    decay_v,
    phase_v,
    count_s,
    slot_s,
    pair_send,
    pair_recv,
    part_send,
    part_recv,
    spec_send,
    spec_recv,
    modal_send,
    modal_recv,
    ret_send,
    ret_recv,
    back_send,
    back_recv,
    back_other,
    fwd_table,
    bwd_table,
    lag_table,
    padded,
    local_sem,
    send_sem,
    recv_sem,
):
    steps, reduced = load_v.shape[0], stress_v.shape[0]
    width = reduced // dofs
    half = reduced // HALVES
    groups = steps // ROWS
    parts = dofs // HALVES
    spacing = sectors // (groups * HALVES)
    mixers = groups * parts
    peers = sectors * parts
    f32, bf16 = jnp.float32, jnp.bfloat16

    own_sector = lax.axis_index("sector")
    own_dof = lax.axis_index("dof")
    own_half = lax.rem(own_dof, HALVES)
    other_half = 1 - own_half
    own_pair = own_dof // HALVES
    me = own_sector * parts + own_pair
    own_place = own_sector // spacing
    own_group = own_place // HALVES
    is_mixer = (lax.rem(own_sector, spacing) == 0) & (lax.rem(own_place, HALVES) == own_half)
    sibling = (own_sector, own_pair * HALVES + other_half)

    def device(index):
        return (index // parts, lax.rem(index, parts) * HALVES + own_half)

    def mixer_of(group, part):
        return (group * HALVES + own_half) * spacing * parts + part

    def load(src, dst, index):
        copy = pltpu.make_async_copy(src, dst, local_sem.at[index])
        copy.start()
        return copy

    def columns_of(which):
        return pl.ds(pl.multiple_of(which * half, 128), half)

    load_copy = load(load_hbm.at[0], load_v, 0)
    other_copy = load(basis_hbm.at[:, columns_of(other_half)], basis_v.at[0], 1)
    own_copy = load(basis_hbm.at[:, columns_of(own_half)], basis_v.at[1], 2)
    slot_copy = load(slot_hbm, slot_s, 3)
    count_copy = load(count_hbm, count_s, 4)
    decay_copy = load(decay_hbm, decay_v, 5)
    phase_copy = load(phase_hbm, phase_v, 6)
    modes_copy = load(modes_hbm.at[0, columns_of(own_half), :], modes_v, 7)
    stress_copy = load(stress_hbm, stress_v, 8)

    barrier = pltpu.get_barrier_semaphore()

    def greet(target):
        pl.semaphore_signal(barrier, inc=1, device_id=target, device_id_type=MESH)

    greet(sibling)

    @pl.when(is_mixer)
    def _():
        each(peers - 1, lambda index: greet(device(lax.rem(me + index + 1, peers))))

    @pl.when(jnp.logical_not(is_mixer))
    def _():
        each(mixers, lambda index: greet(device(mixer_of(index // parts, index % parts))))

    def remote(src, dst, index, target):
        return pltpu.make_async_remote_copy(
            src_ref=src,
            dst_ref=dst,
            send_sem=send_sem.at[index],
            recv_sem=recv_sem.at[index],
            device_id=target,
            device_id_type=MESH,
        )

    def send_to(src, dst, index, target):
        @pl.when(target != me)
        def _():
            remote(src, dst, index, device(target)).start()

        @pl.when(target == me)
        def _():
            pltpu.make_async_copy(src, dst, recv_sem.at[index]).start()

    def arrived(ref, index):
        pltpu.make_async_copy(ref, ref, recv_sem.at[index]).wait()

    load_copy.wait()
    other_copy.wait()
    pair_send[...] = jnp.dot(load_v[...], basis_v[0], preferred_element_type=f32).astype(bf16)

    @pl.when(is_mixer)
    def _():
        pl.semaphore_wait(barrier, peers)

    @pl.when(jnp.logical_not(is_mixer))
    def _():
        pl.semaphore_wait(barrier, mixers + 1)

    pair_copy = remote(pair_send, pair_recv, 0, sibling)
    pair_copy.start()
    own_copy.wait()
    product = jnp.dot(load_v[...], basis_v[1], preferred_element_type=f32)
    pair_copy.wait_recv()
    summed = (product + pair_recv[...].astype(f32)).astype(bf16)
    for part in range(parts):
        part_send[part] = summed[:, part * width : (part + 1) * width].reshape(
            groups, ROWS, width
        )
    for part in range(parts):
        for group in range(groups):
            send_to(
                part_send.at[part, group],
                part_recv.at[own_sector, own_pair],
                1,
                mixer_of(group, part),
            )

    slot_copy.wait()
    count_copy.wait()
    decay_copy.wait()
    phase_copy.wait()

    @pl.when(is_mixer)
    def _():
        wide = sectors * ROWS
        row = lax.broadcasted_iota(jnp.int32, (sectors, wide), 0)
        sector = (lax.broadcasted_iota(jnp.int32, (sectors, wide), 1) // ROWS).astype(f32)
        harmonic = jnp.zeros((sectors, wide), f32)
        for slot in range(sectors):
            harmonic = jnp.where(row == slot, slot_s[slot].astype(f32), harmonic)
        middle = float(sectors // 2)
        sine = harmonic > middle
        order = jnp.where(sine, harmonic - middle, harmonic)
        turns = order * sector
        residue = turns - float(sectors) * jnp.floor(turns * (1.0 / sectors))
        angle = residue * jnp.float32(2.0 * math.pi / sectors)
        wave = jnp.cos(angle - jnp.where(sine, jnp.float32(0.5 * math.pi), jnp.float32(0.0)))
        single = (harmonic == 0.0) | (harmonic == middle)
        weight = jnp.where(
            single, jnp.float32(math.sqrt(1.0 / sectors)), jnp.float32(math.sqrt(2.0 / sectors))
        )
        small = weight * wave
        table = jnp.broadcast_to(small[:, None, :], (sectors, ROWS, wide)).reshape(wide, wide)
        left = lax.broadcasted_iota(jnp.int32, (wide, wide), 0) % ROWS
        right = lax.broadcasted_iota(jnp.int32, (wide, wide), 1) % ROWS
        table = jnp.where(left == right, table, 0.0)
        for where_to, values in ((fwd_table, table), (bwd_table, table.T)):
            high = values.astype(bf16)
            where_to[0] = high
            where_to[1] = (values - high.astype(f32)).astype(bf16)

    def mix(table_ref, values):
        return (
            jnp.dot(table_ref[0], values, preferred_element_type=f32)
            + jnp.dot(table_ref[1], values, preferred_element_type=f32)
        ).astype(bf16)

    def spread(source, sink, which):
        dst = sink.at[own_group, :, pl.ds(pl.multiple_of(own_pair * width, 128), width)]

        def send(index):
            target = lax.rem(me + index + 1, peers)
            remote(source.at[target // parts], dst, which, device(target)).start()

        each(peers - 1, send)
        pltpu.make_async_copy(source.at[own_sector], dst, recv_sem.at[which]).start()

    @pl.when(is_mixer)
    def _():
        arrived(part_recv, 1)
        total = part_recv[:, 0].astype(f32)
        for pair in range(1, parts):
            total = total + part_recv[:, pair].astype(f32)
        values = total.reshape(sectors * ROWS, width).astype(bf16)
        spec_send[...] = mix(fwd_table, values).reshape(sectors, ROWS, width)
        spread(spec_send, spec_recv, 2)

    decay = decay_v[...]
    lag = lax.broadcasted_iota(jnp.int32, lag_table.shape, 0).astype(f32)
    gain = jnp.sqrt(1.0 - jnp.exp(-2.0 * decay))
    lag_table[...] = gain * jnp.exp(-decay * lag) * jnp.cos(phase_v[...] * lag)
    padded[pl.ds(0, steps), :] = jnp.zeros((steps, padded.shape[1]), f32)

    modes_copy.wait()
    arrived(spec_recv, 2)
    modal_send[...] = jnp.dot(
        spec_recv[...].reshape(steps, half), modes_v[...], preferred_element_type=f32
    )
    modal_copy = remote(modal_send, modal_recv, 3, sibling)
    modal_copy.start()
    modal_copy.wait_recv()
    modal = modal_send[...] + modal_recv[...]
    mode = lax.broadcasted_iota(jnp.int32, modal.shape, 1)
    padded[pl.ds(steps, steps), :] = jnp.where(mode < count_s[0], modal, 0.0)
    cut = steps // 2
    upper = jnp.zeros((cut, modal.shape[1]), f32)
    lower = jnp.zeros((cut, modal.shape[1]), f32)
    for n in range(steps):
        scale = lag_table[pl.ds(n, 1), :]
        if n < cut:
            upper = upper + scale * padded[pl.ds(steps - n, cut), :]
        lower = lower + scale * padded[pl.ds(steps + cut - n, cut), :]
    response = jnp.concatenate([upper, lower], axis=0).astype(bf16)
    own_rows = modes_v[pl.ds(pl.multiple_of(own_pair * width, 128), width), :]
    returned = lax.dot_general(
        response, own_rows, (((1,), (1,)), ((), ())), preferred_element_type=f32
    )
    ret_send[...] = returned.astype(bf16).reshape(groups, ROWS, width)
    for group in range(groups):
        send_to(ret_send.at[group], ret_recv.at[own_sector], 4, mixer_of(group, own_pair))

    @pl.when(is_mixer)
    def _():
        arrived(ret_recv, 4)
        values = ret_recv[...].reshape(sectors * ROWS, width)
        back_send[...] = mix(bwd_table, values).reshape(sectors, ROWS, width)
        spread(back_send, back_recv, 5)

    stress_copy.wait()
    arrived(back_recv, 5)
    back_copy = remote(back_recv, back_other, 6, sibling)
    back_copy.start()

    def rows_of(which):
        return stress_v[pl.ds(pl.multiple_of(which * half, 128), half), :]

    field = jnp.dot(
        back_recv[...].reshape(steps, half), rows_of(own_half), preferred_element_type=f32
    )
    back_copy.wait_recv()
    field = field + jnp.dot(
        back_other[...].reshape(steps, half), rows_of(other_half), preferred_element_type=f32
    )
    out_ref[0] = field.astype(bf16)

    def sent(ref, index):
        pltpu.make_async_copy(ref, ref, send_sem.at[index]).wait()

    pair_copy.wait_send()
    modal_copy.wait_send()
    back_copy.wait_send()

    @pl.when(is_mixer)
    def _():
        for part in range(parts):
            sent(part_send.at[part, pl.ds(0, groups - (part == 0))], 1)
        for index in (2, 5):
            sent(part_recv.at[pl.ds(0, sectors - 1)], index)
            if parts > 1:
                sent(part_recv.at[0, pl.ds(0, parts - 1)], index)
        sent(ret_send.at[pl.ds(0, groups - 1)], 4)

    @pl.when(jnp.logical_not(is_mixer))
    def _():
        sent(part_send, 1)
        sent(ret_send, 4)


def local(
    sectors,
    dofs,
    load_history,
    sector_basis,
    harmonic_modes,
    stress_basis,
    mode_decay,
    mode_phase,
    mode_count,
    slot_harmonic,
):
    _, steps, rows = load_history.shape
    reduced = sector_basis.shape[1]
    modes = harmonic_modes.shape[2]
    stress = stress_basis.shape[1]
    width = reduced // dofs
    groups = steps // ROWS
    parts = dofs // HALVES
    half = reduced // HALVES
    wide = sectors * ROWS
    bf16, f32 = jnp.bfloat16, jnp.float32
    flops = 2 * steps * reduced * (rows + stress + 2 * modes)
    return pl.pallas_call(
        functools.partial(kernel, sectors, dofs),
        out_shape=jax.ShapeDtypeStruct((1, steps, stress), bf16),
        in_specs=[pl.BlockSpec(memory_space=pltpu.HBM)] * 8,
        out_specs=pl.BlockSpec(memory_space=pltpu.VMEM),
        scratch_shapes=[
            pltpu.VMEM((steps, rows), bf16),
            pltpu.VMEM((HALVES, rows, half), bf16),
            pltpu.VMEM((half, modes), bf16),
            pltpu.VMEM((reduced, stress), bf16),
            pltpu.VMEM(mode_decay.shape, f32),
            pltpu.VMEM(mode_phase.shape, f32),
            pltpu.SMEM(mode_count.shape, jnp.int32),
            pltpu.SMEM(slot_harmonic.shape, jnp.int32),
            pltpu.VMEM((steps, half), bf16),
            pltpu.VMEM((steps, half), bf16),
            pltpu.VMEM((parts, groups, ROWS, width), bf16),
            pltpu.VMEM((sectors, parts, ROWS, width), bf16),
            pltpu.VMEM((sectors, ROWS, width), bf16),
            pltpu.VMEM((groups, ROWS, half), bf16),
            pltpu.VMEM((steps, modes), f32),
            pltpu.VMEM((steps, modes), f32),
            pltpu.VMEM((groups, ROWS, width), bf16),
            pltpu.VMEM((sectors, ROWS, width), bf16),
            pltpu.VMEM((sectors, ROWS, width), bf16),
            pltpu.VMEM((groups, ROWS, half), bf16),
            pltpu.VMEM((groups, ROWS, half), bf16),
            pltpu.VMEM((2, wide, wide), bf16),
            pltpu.VMEM((2, wide, wide), bf16),
            pltpu.VMEM((steps, modes), f32),
            pltpu.VMEM((2 * steps, modes), f32),
            pltpu.SemaphoreType.DMA((9,)),
            pltpu.SemaphoreType.DMA((7,)),
            pltpu.SemaphoreType.DMA((7,)),
        ],
        compiler_params=pltpu.CompilerParams(
            collective_id=0, has_side_effects=True, vmem_limit_bytes=60 * 1024 * 1024
        ),
        cost_estimate=pl.CostEstimate(
            flops=flops, bytes_accessed=2 * reduced * (rows + stress), transcendentals=0
        ),
    )(
        load_history,
        sector_basis,
        harmonic_modes,
        stress_basis,
        mode_decay,
        mode_phase,
        mode_count,
        slot_harmonic,
    )


def solution(mesh):
    return jax.shard_map(
        functools.partial(local, mesh.shape["sector"], mesh.shape["dof"]),
        mesh=mesh,
        in_specs=(
            P("sector", None, "dof"),
            P("dof", None),
            P("sector", None, None),
            P(None, "dof"),
            P("sector", None),
            P("sector", None),
            P("sector"),
            P(),
        ),
        out_specs=P("sector", None, "dof"),
        check_vma=False,
    )
```

```python
import functools
import math

import jax
import jax.numpy as jnp
from jax import lax
from jax.experimental import pallas as pl
from jax.experimental.pallas import tpu as pltpu
from jax.sharding import PartitionSpec as P

MESH = pl.DeviceIdType.MESH
ROWS = 16
HALVES = 2
CHUNKS = 3


def each(count, body):
    if count <= 32:
        for index in range(count):
            body(index)
    else:

        @pl.loop(0, count)
        def _(index):
            body(index)


def kernel(
    sectors,
    dofs,
    load_hbm,
    basis_hbm,
    modes_hbm,
    stress_hbm,
    decay_hbm,
    phase_hbm,
    count_hbm,
    slot_hbm,
    out_ref,
    load_v,
    basis_v,
    modes_v,
    stress_v,
    decay_v,
    phase_v,
    count_s,
    slot_s,
    pair_send,
    pair_recv,
    part_send,
    part_recv,
    spec_send,
    spec_recv,
    modal_send,
    modal_recv,
    ret_send,
    ret_recv,
    back_send,
    back_recv,
    back_other,
    fwd_table,
    bwd_table,
    power_real,
    power_imag,
    local_sem,
    send_sem,
    recv_sem,
):
    steps, reduced = load_v.shape[0], stress_v.shape[0]
    width = reduced // dofs
    half = reduced // HALVES
    groups = steps // ROWS
    parts = dofs // HALVES
    spacing = sectors // (groups * HALVES)
    mixers = groups * parts
    peers = sectors * parts
    f32, bf16 = jnp.float32, jnp.bfloat16

    own_sector = lax.axis_index("sector")
    own_dof = lax.axis_index("dof")
    own_half = lax.rem(own_dof, HALVES)
    other_half = 1 - own_half
    own_pair = own_dof // HALVES
    me = own_sector * parts + own_pair
    own_place = own_sector // spacing
    own_group = own_place // HALVES
    is_mixer = (lax.rem(own_sector, spacing) == 0) & (lax.rem(own_place, HALVES) == own_half)
    sibling = (own_sector, own_pair * HALVES + other_half)

    def device(index):
        return (index // parts, lax.rem(index, parts) * HALVES + own_half)

    def mixer_of(group, part):
        return (group * HALVES + own_half) * spacing * parts + part

    def load(src, dst, index):
        copy = pltpu.make_async_copy(src, dst, local_sem.at[index])
        copy.start()
        return copy

    def columns_of(which):
        return pl.ds(pl.multiple_of(which * half, 128), half)

    load_copy = load(load_hbm.at[0], load_v, 0)
    chunk = load_v.shape[1] // CHUNKS
    basis_copies = [
        [
            load(
                basis_hbm.at[pl.ds(index * chunk, chunk), columns_of(which)],
                basis_v.at[turn, pl.ds(index * chunk, chunk)],
                7 + turn * CHUNKS + index,
            )
            for index in range(CHUNKS)
        ]
        for turn, which in enumerate((other_half, own_half))
    ]

    def partial_product(turn):
        total = None
        for index in range(CHUNKS):
            rows = pl.ds(index * chunk, chunk)
            basis_copies[turn][index].wait()
            term = jnp.dot(load_v[:, rows], basis_v[turn, rows, :], preferred_element_type=f32)
            total = term if total is None else total + term
        return total

    barrier = pltpu.get_barrier_semaphore()

    def greet(target):
        pl.semaphore_signal(barrier, inc=1, device_id=target, device_id_type=MESH)

    greet(sibling)

    @pl.when(is_mixer)
    def _():
        each(peers - 1, lambda index: greet(device(lax.rem(me + index + 1, peers))))

    @pl.when(jnp.logical_not(is_mixer))
    def _():
        each(mixers, lambda index: greet(device(mixer_of(index // parts, index % parts))))

    def remote(src, dst, index, target):
        return pltpu.make_async_remote_copy(
            src_ref=src,
            dst_ref=dst,
            send_sem=send_sem.at[index],
            recv_sem=recv_sem.at[index],
            device_id=target,
            device_id_type=MESH,
        )

    def send_to(src, dst, index, target):
        @pl.when(target != me)
        def _():
            remote(src, dst, index, device(target)).start()

        @pl.when(target == me)
        def _():
            pltpu.make_async_copy(src, dst, recv_sem.at[index]).start()

    def arrived(ref, index):
        pltpu.make_async_copy(ref, ref, recv_sem.at[index]).wait()

    load_copy.wait()
    pair_send[...] = partial_product(0).astype(bf16)

    @pl.when(is_mixer)
    def _():
        pl.semaphore_wait(barrier, peers)

    @pl.when(jnp.logical_not(is_mixer))
    def _():
        pl.semaphore_wait(barrier, mixers + 1)

    pair_copy = remote(pair_send, pair_recv, 0, sibling)
    pair_copy.start()
    product = partial_product(1)
    slot_copy = load(slot_hbm, slot_s, 1)
    count_copy = load(count_hbm, count_s, 2)
    decay_copy = load(decay_hbm, decay_v, 3)
    phase_copy = load(phase_hbm, phase_v, 4)
    modes_copy = load(modes_hbm.at[0, columns_of(own_half), :], modes_v, 5)
    stress_copy = load(stress_hbm, stress_v, 6)
    pair_copy.wait_recv()
    summed = (product + pair_recv[...].astype(f32)).astype(bf16)
    for part in range(parts):
        part_send[part] = summed[:, part * width : (part + 1) * width].reshape(
            groups, ROWS, width
        )
    for part in range(parts):
        for group in range(groups):
            send_to(
                part_send.at[part, group],
                part_recv.at[own_sector, own_pair],
                1,
                mixer_of(group, part),
            )

    slot_copy.wait()
    count_copy.wait()
    decay_copy.wait()
    phase_copy.wait()

    @pl.when(is_mixer)
    def _():
        wide = sectors * ROWS
        row = lax.broadcasted_iota(jnp.int32, (sectors, wide), 0)
        sector = (lax.broadcasted_iota(jnp.int32, (sectors, wide), 1) // ROWS).astype(f32)
        harmonic = jnp.zeros((sectors, wide), f32)
        for slot in range(sectors):
            harmonic = jnp.where(row == slot, slot_s[slot].astype(f32), harmonic)
        middle = float(sectors // 2)
        sine = harmonic > middle
        order = jnp.where(sine, harmonic - middle, harmonic)
        turns = order * sector
        residue = turns - float(sectors) * jnp.floor(turns * (1.0 / sectors))
        angle = residue * jnp.float32(2.0 * math.pi / sectors)
        wave = jnp.cos(angle - jnp.where(sine, jnp.float32(0.5 * math.pi), jnp.float32(0.0)))
        single = (harmonic == 0.0) | (harmonic == middle)
        weight = jnp.where(
            single, jnp.float32(math.sqrt(1.0 / sectors)), jnp.float32(math.sqrt(2.0 / sectors))
        )
        small = weight * wave
        table = jnp.broadcast_to(small[:, None, :], (sectors, ROWS, wide)).reshape(wide, wide)
        left = lax.broadcasted_iota(jnp.int32, (wide, wide), 0) % ROWS
        right = lax.broadcasted_iota(jnp.int32, (wide, wide), 1) % ROWS
        table = jnp.where(left == right, table, 0.0)
        for where_to, values in ((fwd_table, table), (bwd_table, table.T)):
            high = values.astype(bf16)
            where_to[0] = high
            where_to[1] = (values - high.astype(f32)).astype(bf16)

    def mix(table_ref, values):
        return (
            jnp.dot(table_ref[0], values, preferred_element_type=f32)
            + jnp.dot(table_ref[1], values, preferred_element_type=f32)
        ).astype(bf16)

    def spread(source, sink, which):
        dst = sink.at[own_group, :, pl.ds(pl.multiple_of(own_pair * width, 128), width)]

        def send(index):
            target = lax.rem(me + index + 1, peers)
            remote(source.at[target // parts], dst, which, device(target)).start()

        each(peers - 1, send)
        pltpu.make_async_copy(source.at[own_sector], dst, recv_sem.at[which]).start()

    @pl.when(is_mixer)
    def _():
        arrived(part_recv, 1)
        total = part_recv[:, 0].astype(f32)
        for pair in range(1, parts):
            total = total + part_recv[:, pair].astype(f32)
        values = total.reshape(sectors * ROWS, width).astype(bf16)
        spec_send[...] = mix(fwd_table, values).reshape(sectors, ROWS, width)
        spread(spec_send, spec_recv, 2)

    decay = decay_v[...]
    gain = jnp.sqrt(1.0 - jnp.exp(-2.0 * decay))
    power = lax.shift_left(1, lax.broadcasted_iota(jnp.int32, power_real.shape, 0)).astype(f32)
    damping = jnp.exp(-decay * power)
    power_real[...] = damping * jnp.cos(phase_v[...] * power)
    power_imag[...] = damping * jnp.sin(phase_v[...] * power)

    modes_copy.wait()
    arrived(spec_recv, 2)
    modal_send[...] = jnp.dot(
        spec_recv[...].reshape(steps, half), modes_v[...], preferred_element_type=f32
    )
    modal_copy = remote(modal_send, modal_recv, 3, sibling)
    modal_copy.start()
    modal_copy.wait_recv()
    modal = modal_send[...] + modal_recv[...]
    mode = lax.broadcasted_iota(jnp.int32, modal.shape, 1)
    real = jnp.where(mode < count_s[0], modal, 0.0)
    imag = None
    step = lax.broadcasted_iota(jnp.int32, modal.shape, 0)

    def later(values, lag):
        if lag % 8 == 0:
            zeros = jnp.zeros((lag, values.shape[1]), f32)
            return jnp.concatenate([zeros, values[: steps - lag]], axis=0)
        return jnp.where(step >= lag, pltpu.roll(values, lag, 0), 0.0)

    for index in range((steps - 1).bit_length()):
        turn_real, turn_imag = power_real[pl.ds(index, 1), :], power_imag[pl.ds(index, 1), :]
        old_real = later(real, 1 << index)
        if imag is None:
            imag = turn_imag * old_real
            real = real + turn_real * old_real
        else:
            old_imag = later(imag, 1 << index)
            real = real + turn_real * old_real - turn_imag * old_imag
            imag = imag + turn_real * old_imag + turn_imag * old_real
    response = (gain * real).astype(bf16)
    own_rows = modes_v[pl.ds(pl.multiple_of(own_pair * width, 128), width), :]
    returned = lax.dot_general(
        response, own_rows, (((1,), (1,)), ((), ())), preferred_element_type=f32
    )
    ret_send[...] = returned.astype(bf16).reshape(groups, ROWS, width)
    for group in range(groups):
        send_to(ret_send.at[group], ret_recv.at[own_sector], 4, mixer_of(group, own_pair))

    @pl.when(is_mixer)
    def _():
        arrived(ret_recv, 4)
        values = ret_recv[...].reshape(sectors * ROWS, width)
        back_send[...] = mix(bwd_table, values).reshape(sectors, ROWS, width)
        spread(back_send, back_recv, 5)

    stress_copy.wait()
    arrived(back_recv, 5)
    back_copy = remote(back_recv, back_other, 6, sibling)
    back_copy.start()

    def rows_of(which):
        return stress_v[pl.ds(pl.multiple_of(which * half, 128), half), :]

    field = jnp.dot(
        back_recv[...].reshape(steps, half), rows_of(own_half), preferred_element_type=f32
    )
    back_copy.wait_recv()
    field = field + jnp.dot(
        back_other[...].reshape(steps, half), rows_of(other_half), preferred_element_type=f32
    )
    out_ref[0] = field

    def sent(ref, index):
        pltpu.make_async_copy(ref, ref, send_sem.at[index]).wait()

    pair_copy.wait_send()
    modal_copy.wait_send()
    back_copy.wait_send()

    @pl.when(is_mixer)
    def _():
        for part in range(parts):
            sent(part_send.at[part, pl.ds(0, groups - (part == 0))], 1)
        for index in (2, 5):
            sent(part_recv.at[pl.ds(0, sectors - 1)], index)
            if parts > 1:
                sent(part_recv.at[0, pl.ds(0, parts - 1)], index)
        sent(ret_send.at[pl.ds(0, groups - 1)], 4)

    @pl.when(jnp.logical_not(is_mixer))
    def _():
        sent(part_send, 1)
        sent(ret_send, 4)


def local(
    sectors,
    dofs,
    load_history,
    sector_basis,
    harmonic_modes,
    stress_basis,
    mode_decay,
    mode_phase,
    mode_count,
    slot_harmonic,
):
    _, steps, rows = load_history.shape
    reduced = sector_basis.shape[1]
    modes = harmonic_modes.shape[2]
    stress = stress_basis.shape[1]
    width = reduced // dofs
    groups = steps // ROWS
    parts = dofs // HALVES
    half = reduced // HALVES
    wide = sectors * ROWS
    bf16, f32 = jnp.bfloat16, jnp.float32
    flops = 2 * steps * reduced * (rows + stress + 2 * modes)
    field = pl.pallas_call(
        functools.partial(kernel, sectors, dofs),
        out_shape=jax.ShapeDtypeStruct((1, steps, stress), f32),
        in_specs=[pl.BlockSpec(memory_space=pltpu.HBM)] * 8,
        out_specs=pl.BlockSpec(memory_space=pltpu.VMEM),
        scratch_shapes=[
            pltpu.VMEM((steps, rows), bf16),
            pltpu.VMEM((HALVES, rows, half), bf16),
            pltpu.VMEM((half, modes), bf16),
            pltpu.VMEM((reduced, stress), bf16),
            pltpu.VMEM(mode_decay.shape, f32),
            pltpu.VMEM(mode_phase.shape, f32),
            pltpu.SMEM(mode_count.shape, jnp.int32),
            pltpu.SMEM(slot_harmonic.shape, jnp.int32),
            pltpu.VMEM((steps, half), bf16),
            pltpu.VMEM((steps, half), bf16),
            pltpu.VMEM((parts, groups, ROWS, width), bf16),
            pltpu.VMEM((sectors, parts, ROWS, width), bf16),
            pltpu.VMEM((sectors, ROWS, width), bf16),
            pltpu.VMEM((groups, ROWS, half), bf16),
            pltpu.VMEM((steps, modes), f32),
            pltpu.VMEM((steps, modes), f32),
            pltpu.VMEM((groups, ROWS, width), bf16),
            pltpu.VMEM((sectors, ROWS, width), bf16),
            pltpu.VMEM((sectors, ROWS, width), bf16),
            pltpu.VMEM((groups, ROWS, half), bf16),
            pltpu.VMEM((groups, ROWS, half), bf16),
            pltpu.VMEM((2, wide, wide), bf16),
            pltpu.VMEM((2, wide, wide), bf16),
            pltpu.VMEM((8, modes), f32),
            pltpu.VMEM((8, modes), f32),
            pltpu.SemaphoreType.DMA((7 + HALVES * CHUNKS,)),
            pltpu.SemaphoreType.DMA((7,)),
            pltpu.SemaphoreType.DMA((7,)),
        ],
        compiler_params=pltpu.CompilerParams(
            collective_id=0, has_side_effects=True, vmem_limit_bytes=60 * 1024 * 1024
        ),
        cost_estimate=pl.CostEstimate(
            flops=flops, bytes_accessed=2 * reduced * (rows + stress), transcendentals=0
        ),
    )(
        load_history,
        sector_basis,
        harmonic_modes,
        stress_basis,
        mode_decay,
        mode_phase,
        mode_count,
        slot_harmonic,
    )
    return field.astype(bf16)


def solution(mesh):
    return jax.shard_map(
        functools.partial(local, mesh.shape["sector"], mesh.shape["dof"]),
        mesh=mesh,
        in_specs=(
            P("sector", None, "dof"),
            P("dof", None),
            P("sector", None, None),
            P(None, "dof"),
            P("sector", None),
            P("sector", None),
            P("sector"),
            P(),
        ),
        out_specs=P("sector", None, "dof"),
        check_vma=False,
    )
```

```python
import functools
import math

import jax
import jax.numpy as jnp
from jax import lax
from jax.experimental import pallas as pl
from jax.experimental.pallas import tpu as pltpu
from jax.sharding import PartitionSpec as P

MESH = pl.DeviceIdType.MESH
ROWS = 16
HALVES = 2
HEAD = 8
CHUNKS = 3


def each(count, body):
    if count <= 32:
        for index in range(count):
            body(index)
    else:

        @pl.loop(0, count)
        def _(index):
            body(index)


def kernel(
    sectors,
    dofs,
    load_hbm,
    basis_hbm,
    modes_hbm,
    stress_hbm,
    small_ref,
    out_ref,
    load_v,
    basis_v,
    modes_v,
    stress_v,
    pair_send,
    pair_recv,
    part_send,
    part_recv,
    spec_send,
    spec_recv,
    modal_send,
    modal_recv,
    ret_send,
    ret_recv,
    back_send,
    back_recv,
    back_other,
    fwd_table,
    bwd_table,
    power_real,
    power_imag,
    local_sem,
    send_sem,
    recv_sem,
):
    steps, reduced = load_v.shape[0], stress_v.shape[0]
    width = reduced // dofs
    half = reduced // HALVES
    groups = steps // ROWS
    parts = dofs // HALVES
    spacing = sectors // (groups * HALVES)
    mixers = groups * parts
    peers = sectors * parts
    f32, bf16 = jnp.float32, jnp.bfloat16

    own_sector = lax.axis_index("sector")
    own_dof = lax.axis_index("dof")
    own_half = lax.rem(own_dof, HALVES)
    other_half = 1 - own_half
    own_pair = own_dof // HALVES
    me = own_sector * parts + own_pair
    own_place = own_sector // spacing
    own_group = own_place // HALVES
    is_mixer = (lax.rem(own_sector, spacing) == 0) & (lax.rem(own_place, HALVES) == own_half)
    sibling = (own_sector, own_pair * HALVES + other_half)

    def device(index):
        return (index // parts, lax.rem(index, parts) * HALVES + own_half)

    def mixer_of(group, part):
        return (group * HALVES + own_half) * spacing * parts + part

    def load(src, dst, index):
        copy = pltpu.make_async_copy(src, dst, local_sem.at[index])
        copy.start()
        return copy

    def columns_of(which):
        return pl.ds(pl.multiple_of(which * half, 128), half)

    load_copy = load(load_hbm.at[0], load_v, 0)
    chunk = load_v.shape[1] // CHUNKS
    basis_copies = [
        [
            load(
                basis_hbm.at[pl.ds(index * chunk, chunk), columns_of(which)],
                basis_v.at[turn, pl.ds(index * chunk, chunk)],
                3 + turn * CHUNKS + index,
            )
            for index in range(CHUNKS)
        ]
        for turn, which in enumerate((other_half, own_half))
    ]

    def partial_product(turn):
        total = None
        for index in range(CHUNKS):
            rows = pl.ds(index * chunk, chunk)
            basis_copies[turn][index].wait()
            term = jnp.dot(load_v[:, rows], basis_v[turn, rows, :], preferred_element_type=f32)
            total = term if total is None else total + term
        return total

    barrier = pltpu.get_barrier_semaphore()

    def greet(target):
        pl.semaphore_signal(barrier, inc=1, device_id=target, device_id_type=MESH)

    greet(sibling)

    @pl.when(is_mixer)
    def _():
        each(peers - 1, lambda index: greet(device(lax.rem(me + index + 1, peers))))

    @pl.when(jnp.logical_not(is_mixer))
    def _():
        each(mixers, lambda index: greet(device(mixer_of(index // parts, index % parts))))

    def remote(src, dst, index, target):
        return pltpu.make_async_remote_copy(
            src_ref=src,
            dst_ref=dst,
            send_sem=send_sem.at[index],
            recv_sem=recv_sem.at[index],
            device_id=target,
            device_id_type=MESH,
        )

    def send_to(src, dst, index, target):
        @pl.when(target != me)
        def _():
            remote(src, dst, index, device(target)).start()

        @pl.when(target == me)
        def _():
            pltpu.make_async_copy(src, dst, recv_sem.at[index]).start()

    def arrived(ref, index):
        pltpu.make_async_copy(ref, ref, recv_sem.at[index]).wait()

    @pl.when(is_mixer)
    def _():
        wide = sectors * ROWS
        sector = (lax.broadcasted_iota(jnp.int32, (sectors, wide), 1) >> (ROWS.bit_length() - 1)).astype(f32)
        harmonic = jnp.broadcast_to(small_ref[pl.ds(HEAD, sectors), 0:1], (sectors, wide))
        middle = float(sectors // 2)
        sine = harmonic > middle
        order = jnp.where(sine, harmonic - middle, harmonic)
        turns = order * sector
        residue = turns - float(sectors) * jnp.floor(turns * (1.0 / sectors))
        angle = residue * jnp.float32(2.0 * math.pi / sectors)
        wave = jnp.cos(angle - jnp.where(sine, jnp.float32(0.5 * math.pi), jnp.float32(0.0)))
        single = (harmonic == 0.0) | (harmonic == middle)
        weight = jnp.where(
            single, jnp.float32(math.sqrt(1.0 / sectors)), jnp.float32(math.sqrt(2.0 / sectors))
        )
        small = weight * wave
        table = jnp.broadcast_to(small[:, None, :], (sectors, ROWS, wide)).reshape(wide, wide)
        left = lax.broadcasted_iota(jnp.int32, (wide, wide), 0) & (ROWS - 1)
        right = lax.broadcasted_iota(jnp.int32, (wide, wide), 1) & (ROWS - 1)
        table = jnp.where(left == right, table, 0.0)
        for where_to, values in ((fwd_table, table), (bwd_table, table.T)):
            high = values.astype(bf16)
            where_to[0] = high
            where_to[1] = (values - high.astype(f32)).astype(bf16)

    decay = small_ref[0:1, :]
    phase = small_ref[1:2, :]
    gain = jnp.sqrt(1.0 - jnp.exp(-2.0 * decay))
    power = lax.shift_left(1, lax.broadcasted_iota(jnp.int32, power_real.shape, 0)).astype(f32)
    damping = jnp.exp(-decay * power)
    power_real[...] = damping * jnp.cos(phase * power)
    power_imag[...] = damping * jnp.sin(phase * power)

    load_copy.wait()
    pair_send[...] = partial_product(0).astype(bf16)

    @pl.when(is_mixer)
    def _():
        pl.semaphore_wait(barrier, peers)

    @pl.when(jnp.logical_not(is_mixer))
    def _():
        pl.semaphore_wait(barrier, mixers + 1)

    pair_copy = remote(pair_send, pair_recv, 0, sibling)
    pair_copy.start()
    product = partial_product(1)
    modes_copy = load(modes_hbm.at[0, columns_of(own_half), :], modes_v, 1)
    stress_copy = load(stress_hbm, stress_v, 2)
    pair_copy.wait_recv()
    summed = (product + pair_recv[...].astype(f32)).astype(bf16)
    for part in range(parts):
        part_send[part] = summed[:, part * width : (part + 1) * width].reshape(
            groups, ROWS, width
        )
    for part in range(parts):
        for group in range(groups):
            send_to(
                part_send.at[part, group],
                part_recv.at[own_sector, own_pair],
                1,
                mixer_of(group, part),
            )

    def mix(table_ref, values):
        return (
            jnp.dot(table_ref[0], values, preferred_element_type=f32)
            + jnp.dot(table_ref[1], values, preferred_element_type=f32)
        ).astype(bf16)

    def spread(source, sink, which):
        dst = sink.at[own_group, :, pl.ds(pl.multiple_of(own_pair * width, 128), width)]

        def send(index):
            target = lax.rem(me + index + 1, peers)
            remote(source.at[target // parts], dst, which, device(target)).start()

        each(peers - 1, send)
        pltpu.make_async_copy(source.at[own_sector], dst, recv_sem.at[which]).start()

    @pl.when(is_mixer)
    def _():
        arrived(part_recv, 1)
        total = part_recv[:, 0].astype(f32)
        for pair in range(1, parts):
            total = total + part_recv[:, pair].astype(f32)
        values = total.reshape(sectors * ROWS, width).astype(bf16)
        spec_send[...] = mix(fwd_table, values).reshape(sectors, ROWS, width)
        spread(spec_send, spec_recv, 2)

    modes_copy.wait()
    arrived(spec_recv, 2)
    modal_send[...] = jnp.dot(
        spec_recv[...].reshape(steps, half), modes_v[...], preferred_element_type=f32
    )
    modal_copy = remote(modal_send, modal_recv, 3, sibling)
    modal_copy.start()
    modal_copy.wait_recv()
    modal = modal_send[...] + modal_recv[...]
    mode = lax.broadcasted_iota(jnp.int32, modal.shape, 1).astype(f32)
    real = jnp.where(mode < small_ref[2:3, :], modal, 0.0)
    imag = None
    step = lax.broadcasted_iota(jnp.int32, modal.shape, 0)

    def later(values, lag):
        if lag % 8 == 0:
            zeros = jnp.zeros((lag, values.shape[1]), f32)
            return jnp.concatenate([zeros, values[: steps - lag]], axis=0)
        return jnp.where(step >= lag, pltpu.roll(values, lag, 0), 0.0)

    for index in range((steps - 1).bit_length()):
        turn_real, turn_imag = power_real[pl.ds(index, 1), :], power_imag[pl.ds(index, 1), :]
        old_real = later(real, 1 << index)
        if imag is None:
            imag = turn_imag * old_real
            real = real + turn_real * old_real
        else:
            old_imag = later(imag, 1 << index)
            real = real + turn_real * old_real - turn_imag * old_imag
            imag = imag + turn_real * old_imag + turn_imag * old_real
    response = (gain * real).astype(bf16)
    own_rows = modes_v[pl.ds(pl.multiple_of(own_pair * width, 128), width), :]
    returned = lax.dot_general(
        response, own_rows, (((1,), (1,)), ((), ())), preferred_element_type=f32
    )
    ret_send[...] = returned.astype(bf16).reshape(groups, ROWS, width)
    for group in range(groups):
        send_to(ret_send.at[group], ret_recv.at[own_sector], 4, mixer_of(group, own_pair))

    @pl.when(is_mixer)
    def _():
        arrived(ret_recv, 4)
        values = ret_recv[...].reshape(sectors * ROWS, width)
        back_send[...] = mix(bwd_table, values).reshape(sectors, ROWS, width)
        spread(back_send, back_recv, 5)

    stress_copy.wait()
    arrived(back_recv, 5)
    back_copy = remote(back_recv, back_other, 6, sibling)
    back_copy.start()

    def rows_of(which):
        return stress_v[pl.ds(pl.multiple_of(which * half, 128), half), :]

    field = jnp.dot(
        back_recv[...].reshape(steps, half), rows_of(own_half), preferred_element_type=f32
    )
    back_copy.wait_recv()
    field = field + jnp.dot(
        back_other[...].reshape(steps, half), rows_of(other_half), preferred_element_type=f32
    )
    out_ref[0] = field.astype(bf16)

    def sent(ref, index):
        pltpu.make_async_copy(ref, ref, send_sem.at[index]).wait()

    pair_copy.wait_send()
    modal_copy.wait_send()
    back_copy.wait_send()

    @pl.when(is_mixer)
    def _():
        for part in range(parts):
            sent(part_send.at[part, pl.ds(0, groups - (part == 0))], 1)
        for index in (2, 5):
            sent(part_recv.at[pl.ds(0, sectors - 1)], index)
            if parts > 1:
                sent(part_recv.at[0, pl.ds(0, parts - 1)], index)
        sent(ret_send.at[pl.ds(0, groups - 1)], 4)

    @pl.when(jnp.logical_not(is_mixer))
    def _():
        sent(part_send, 1)
        sent(ret_send, 4)


def local(
    sectors,
    dofs,
    load_history,
    sector_basis,
    harmonic_modes,
    stress_basis,
    mode_decay,
    mode_phase,
    mode_count,
    slot_harmonic,
):
    _, steps, rows = load_history.shape
    reduced = sector_basis.shape[1]
    modes = harmonic_modes.shape[2]
    stress = stress_basis.shape[1]
    width = reduced // dofs
    groups = steps // ROWS
    parts = dofs // HALVES
    half = reduced // HALVES
    wide = sectors * ROWS
    bf16, f32 = jnp.bfloat16, jnp.float32
    row = jnp.arange(HEAD + sectors, dtype=jnp.int32)[:, None]
    numbers = jnp.where(row == 2, mode_count[0], jnp.pad(slot_harmonic, (HEAD, 0))[:, None])
    small = jnp.where(
        row == 0, mode_decay, jnp.where(row == 1, mode_phase, numbers.astype(f32))
    )
    flops = 2 * steps * reduced * (rows + stress + 2 * modes)
    return pl.pallas_call(
        functools.partial(kernel, sectors, dofs),
        out_shape=jax.ShapeDtypeStruct((1, steps, stress), bf16),
        in_specs=[pl.BlockSpec(memory_space=pltpu.HBM)] * 4
        + [pl.BlockSpec(memory_space=pltpu.VMEM)],
        out_specs=pl.BlockSpec(memory_space=pltpu.VMEM),
        scratch_shapes=[
            pltpu.VMEM((steps, rows), bf16),
            pltpu.VMEM((HALVES, rows, half), bf16),
            pltpu.VMEM((half, modes), bf16),
            pltpu.VMEM((reduced, stress), bf16),
            pltpu.VMEM((steps, half), bf16),
            pltpu.VMEM((steps, half), bf16),
            pltpu.VMEM((parts, groups, ROWS, width), bf16),
            pltpu.VMEM((sectors, parts, ROWS, width), bf16),
            pltpu.VMEM((sectors, ROWS, width), bf16),
            pltpu.VMEM((groups, ROWS, half), bf16),
            pltpu.VMEM((steps, modes), f32),
            pltpu.VMEM((steps, modes), f32),
            pltpu.VMEM((groups, ROWS, width), bf16),
            pltpu.VMEM((sectors, ROWS, width), bf16),
            pltpu.VMEM((sectors, ROWS, width), bf16),
            pltpu.VMEM((groups, ROWS, half), bf16),
            pltpu.VMEM((groups, ROWS, half), bf16),
            pltpu.VMEM((2, wide, wide), bf16),
            pltpu.VMEM((2, wide, wide), bf16),
            pltpu.VMEM((8, modes), f32),
            pltpu.VMEM((8, modes), f32),
            pltpu.SemaphoreType.DMA((3 + HALVES * CHUNKS,)),
            pltpu.SemaphoreType.DMA((7,)),
            pltpu.SemaphoreType.DMA((7,)),
        ],
        compiler_params=pltpu.CompilerParams(
            collective_id=0, has_side_effects=True, vmem_limit_bytes=54980 * 1024
        ),
        cost_estimate=pl.CostEstimate(
            flops=flops, bytes_accessed=2 * reduced * (rows + stress), transcendentals=0
        ),
    )(
        load_history,
        sector_basis,
        harmonic_modes,
        stress_basis,
        small,
    )


def solution(mesh):
    return jax.shard_map(
        functools.partial(local, mesh.shape["sector"], mesh.shape["dof"]),
        mesh=mesh,
        in_specs=(
            P("sector", None, "dof"),
            P("dof", None),
            P("sector", None, None),
            P(None, "dof"),
            P("sector", None),
            P("sector", None),
            P("sector"),
            P(),
        ),
        out_specs=P("sector", None, "dof"),
        check_vma=False,
    )
```

```python
import functools
import math

import jax
import jax.numpy as jnp
from jax import lax
from jax.experimental import pallas as pl
from jax.experimental.pallas import tpu as pltpu
from jax.sharding import PartitionSpec as P

MESH = pl.DeviceIdType.MESH
ROWS = 16
HALVES = 2
CHUNKS = 3


def each(count, body):
    if count <= 32:
        for index in range(count):
            body(index)
    else:

        @pl.loop(0, count)
        def _(index):
            body(index)


def farthest_first(count):
    return sorted(range(count), key=lambda offset: -min(offset, count - offset))


def kernel(
    sectors,
    dofs,
    load_hbm,
    basis_hbm,
    modes_hbm,
    stress_hbm,
    decay_hbm,
    phase_hbm,
    count_hbm,
    slot_hbm,
    out_ref,
    load_v,
    basis_v,
    modes_v,
    stress_v,
    decay_v,
    phase_v,
    count_s,
    slot_s,
    pair_send,
    pair_recv,
    part_send,
    part_recv,
    spec_send,
    spec_recv,
    modal_send,
    modal_recv,
    ret_send,
    ret_recv,
    back_send,
    back_recv,
    back_other,
    fwd_table,
    bwd_table,
    power_real,
    power_imag,
    local_sem,
    send_sem,
    recv_sem,
):
    steps, reduced = load_v.shape[0], stress_v.shape[0]
    width = reduced // dofs
    half = reduced // HALVES
    groups = steps // ROWS
    parts = dofs // HALVES
    spacing = sectors // (groups * HALVES)
    mixers = groups * parts
    peers = sectors * parts
    f32, bf16 = jnp.float32, jnp.bfloat16

    own_sector = lax.axis_index("sector")
    own_dof = lax.axis_index("dof")
    own_half = lax.rem(own_dof, HALVES)
    other_half = 1 - own_half
    own_pair = own_dof // HALVES
    me = own_sector * parts + own_pair
    own_place = own_sector // spacing
    own_group = own_place // HALVES
    is_mixer = (lax.rem(own_sector, spacing) == 0) & (lax.rem(own_place, HALVES) == own_half)
    sibling = (own_sector, own_pair * HALVES + other_half)

    def device(index):
        return (index // parts, lax.rem(index, parts) * HALVES + own_half)

    def mixer_of(group, part):
        return (group * HALVES + own_half) * spacing * parts + part

    def load(src, dst, index):
        copy = pltpu.make_async_copy(src, dst, local_sem.at[index])
        copy.start()
        return copy

    def columns_of(which):
        return pl.ds(pl.multiple_of(which * half, 128), half)

    slot_copy = load(slot_hbm, slot_s, 1)
    count_copy = load(count_hbm, count_s, 2)
    decay_copy = load(decay_hbm, decay_v, 3)
    phase_copy = load(phase_hbm, phase_v, 4)
    load_copy = load(load_hbm.at[0], load_v, 0)
    chunk = load_v.shape[1] // CHUNKS
    basis_copies = [
        [
            load(
                basis_hbm.at[pl.ds(index * chunk, chunk), columns_of(which)],
                basis_v.at[turn, pl.ds(index * chunk, chunk)],
                7 + turn * CHUNKS + index,
            )
            for index in range(CHUNKS)
        ]
        for turn, which in enumerate((other_half, own_half))
    ]

    def partial_product(turn):
        total = None
        for index in range(CHUNKS):
            rows = pl.ds(index * chunk, chunk)
            basis_copies[turn][index].wait()
            term = jnp.dot(load_v[:, rows], basis_v[turn, rows, :], preferred_element_type=f32)
            total = term if total is None else total + term
        return total

    barrier = pltpu.get_barrier_semaphore()

    def greet(target):
        pl.semaphore_signal(barrier, inc=1, device_id=target, device_id_type=MESH)

    greet(sibling)

    @pl.when(is_mixer)
    def _():
        each(peers - 1, lambda index: greet(device(lax.rem(me + index + 1, peers))))

    @pl.when(jnp.logical_not(is_mixer))
    def _():
        each(mixers, lambda index: greet(device(mixer_of(index // parts, index % parts))))

    def remote(src, dst, index, target):
        return pltpu.make_async_remote_copy(
            src_ref=src,
            dst_ref=dst,
            send_sem=send_sem.at[index],
            recv_sem=recv_sem.at[index],
            device_id=target,
            device_id_type=MESH,
        )

    def send_to(src, dst, index, target):
        @pl.when(target != me)
        def _():
            remote(src, dst, index, device(target)).start()

        @pl.when(target == me)
        def _():
            pltpu.make_async_copy(src, dst, recv_sem.at[index]).start()

    def arrived(ref, index):
        pltpu.make_async_copy(ref, ref, recv_sem.at[index]).wait()

    slot_copy.wait()
    count_copy.wait()
    decay_copy.wait()
    phase_copy.wait()

    @pl.when(is_mixer)
    def _():
        wide = sectors * ROWS
        row = lax.broadcasted_iota(jnp.int32, (sectors, wide), 0)
        sector = (lax.broadcasted_iota(jnp.int32, (sectors, wide), 1) >> (ROWS.bit_length() - 1)).astype(f32)
        harmonic = jnp.zeros((sectors, wide), f32)
        for slot in range(sectors):
            harmonic = jnp.where(row == slot, slot_s[slot].astype(f32), harmonic)
        middle = float(sectors // 2)
        sine = harmonic > middle
        order = jnp.where(sine, harmonic - middle, harmonic)
        turns = order * sector
        residue = turns - float(sectors) * jnp.floor(turns * (1.0 / sectors))
        angle = residue * jnp.float32(2.0 * math.pi / sectors)
        wave = jnp.cos(angle - jnp.where(sine, jnp.float32(0.5 * math.pi), jnp.float32(0.0)))
        single = (harmonic == 0.0) | (harmonic == middle)
        weight = jnp.where(
            single, jnp.float32(math.sqrt(1.0 / sectors)), jnp.float32(math.sqrt(2.0 / sectors))
        )
        small = weight * wave
        table = jnp.broadcast_to(small[:, None, :], (sectors, ROWS, wide)).reshape(wide, wide)
        left = lax.broadcasted_iota(jnp.int32, (wide, wide), 0) & (ROWS - 1)
        right = lax.broadcasted_iota(jnp.int32, (wide, wide), 1) & (ROWS - 1)
        table = jnp.where(left == right, table, 0.0)
        for where_to, values in ((fwd_table, table), (bwd_table, table.T)):
            high = values.astype(bf16)
            where_to[0] = high
            where_to[1] = (values - high.astype(f32)).astype(bf16)

    decay = decay_v[...]
    gain = jnp.sqrt(1.0 - jnp.exp(-2.0 * decay))
    power = lax.shift_left(1, lax.broadcasted_iota(jnp.int32, power_real.shape, 0)).astype(f32)
    damping = jnp.exp(-decay * power)
    power_real[...] = damping * jnp.cos(phase_v[...] * power)
    power_imag[...] = damping * jnp.sin(phase_v[...] * power)

    load_copy.wait()
    pair_send[...] = partial_product(0).astype(bf16)

    @pl.when(is_mixer)
    def _():
        pl.semaphore_wait(barrier, peers)

    @pl.when(jnp.logical_not(is_mixer))
    def _():
        pl.semaphore_wait(barrier, mixers + 1)

    pair_copy = remote(pair_send, pair_recv, 0, sibling)
    pair_copy.start()
    product = partial_product(1)
    modes_copy = load(modes_hbm.at[0, columns_of(own_half), :], modes_v, 5)
    stress_copy = load(stress_hbm, stress_v, 6)
    pair_copy.wait_recv()
    summed = (product + pair_recv[...].astype(f32)).astype(bf16)
    for part in range(parts):
        part_send[part] = summed[:, part * width : (part + 1) * width].reshape(
            groups, ROWS, width
        )
    for offset in farthest_first(groups):
        group = lax.rem(own_group + offset, groups)
        for part in range(parts):
            send_to(
                part_send.at[part, group],
                part_recv.at[own_sector, own_pair],
                1,
                mixer_of(group, part),
            )

    def mix(table_ref, values):
        return (
            jnp.dot(table_ref[0], values, preferred_element_type=f32)
            + jnp.dot(table_ref[1], values, preferred_element_type=f32)
        ).astype(bf16)

    def spread(source, sink, which):
        dst = sink.at[own_group, :, pl.ds(pl.multiple_of(own_pair * width, 128), width)]

        def send(index):
            swing = (index + 1) // 2
            target = lax.rem(me + peers // 2 + (1 - index % 2 * 2) * swing, peers)
            remote(source.at[target // parts], dst, which, device(target)).start()

        each(peers - 1, send)
        pltpu.make_async_copy(source.at[own_sector], dst, recv_sem.at[which]).start()

    @pl.when(is_mixer)
    def _():
        arrived(part_recv, 1)
        total = part_recv[:, 0].astype(f32)
        for pair in range(1, parts):
            total = total + part_recv[:, pair].astype(f32)
        values = total.reshape(sectors * ROWS, width).astype(bf16)
        spec_send[...] = mix(fwd_table, values).reshape(sectors, ROWS, width)
        spread(spec_send, spec_recv, 2)

    modes_copy.wait()
    arrived(spec_recv, 2)
    modal_send[...] = jnp.dot(
        spec_recv[...].reshape(steps, half), modes_v[...], preferred_element_type=f32
    )
    modal_copy = remote(modal_send, modal_recv, 3, sibling)
    modal_copy.start()
    modal_copy.wait_recv()
    modal = modal_send[...] + modal_recv[...]
    mode = lax.broadcasted_iota(jnp.int32, modal.shape, 1)
    real = jnp.where(mode < count_s[0, 0], modal, 0.0)
    imag = None
    step = lax.broadcasted_iota(jnp.int32, modal.shape, 0)

    def later(values, lag):
        if lag % 8 == 0:
            zeros = jnp.zeros((lag, values.shape[1]), f32)
            return jnp.concatenate([zeros, values[: steps - lag]], axis=0)
        return jnp.where(step >= lag, pltpu.roll(values, lag, 0), 0.0)

    for index in range((steps - 1).bit_length()):
        turn_real, turn_imag = power_real[pl.ds(index, 1), :], power_imag[pl.ds(index, 1), :]
        old_real = later(real, 1 << index)
        if imag is None:
            imag = turn_imag * old_real
            real = real + turn_real * old_real
        else:
            old_imag = later(imag, 1 << index)
            real = real + turn_real * old_real - turn_imag * old_imag
            imag = imag + turn_real * old_imag + turn_imag * old_real
    response = (gain * real).astype(bf16)
    own_rows = modes_v[pl.ds(pl.multiple_of(own_pair * width, 128), width), :]
    returned = lax.dot_general(
        response, own_rows, (((1,), (1,)), ((), ())), preferred_element_type=f32
    )
    ret_send[...] = returned.astype(bf16).reshape(groups, ROWS, width)
    for offset in farthest_first(groups):
        group = lax.rem(own_group + offset, groups)
        send_to(ret_send.at[group], ret_recv.at[own_sector], 4, mixer_of(group, own_pair))

    @pl.when(is_mixer)
    def _():
        arrived(ret_recv, 4)
        values = ret_recv[...].reshape(sectors * ROWS, width)
        back_send[...] = mix(bwd_table, values).reshape(sectors, ROWS, width)
        spread(back_send, back_recv, 5)

    stress_copy.wait()
    arrived(back_recv, 5)
    back_copy = remote(back_recv, back_other, 6, sibling)
    back_copy.start()

    def rows_of(which):
        return stress_v[pl.ds(pl.multiple_of(which * half, 128), half), :]

    field = jnp.dot(
        back_recv[...].reshape(steps, half), rows_of(own_half), preferred_element_type=f32
    )
    back_copy.wait_recv()
    field = field + jnp.dot(
        back_other[...].reshape(steps, half), rows_of(other_half), preferred_element_type=f32
    )
    out_ref[0] = field.astype(bf16)

    def sent(ref, index):
        pltpu.make_async_copy(ref, ref, send_sem.at[index]).wait()

    pair_copy.wait_send()
    modal_copy.wait_send()
    back_copy.wait_send()

    @pl.when(is_mixer)
    def _():
        for part in range(parts):
            sent(part_send.at[part, pl.ds(0, groups - (part == 0))], 1)
        for index in (2, 5):
            sent(part_recv.at[pl.ds(0, sectors - 1)], index)
            if parts > 1:
                sent(part_recv.at[0, pl.ds(0, parts - 1)], index)
        sent(ret_send.at[pl.ds(0, groups - 1)], 4)

    @pl.when(jnp.logical_not(is_mixer))
    def _():
        sent(part_send, 1)
        sent(ret_send, 4)


def local(
    sectors,
    dofs,
    load_history,
    sector_basis,
    harmonic_modes,
    stress_basis,
    mode_decay,
    mode_phase,
    mode_count,
    slot_harmonic,
):
    _, steps, rows = load_history.shape
    reduced = sector_basis.shape[1]
    modes = harmonic_modes.shape[2]
    stress = stress_basis.shape[1]
    width = reduced // dofs
    groups = steps // ROWS
    parts = dofs // HALVES
    half = reduced // HALVES
    wide = sectors * ROWS
    bf16, f32 = jnp.bfloat16, jnp.float32
    flops = 2 * steps * reduced * (rows + stress + 2 * modes)
    return pl.pallas_call(
        functools.partial(kernel, sectors, dofs),
        out_shape=jax.ShapeDtypeStruct((1, steps, stress), bf16),
        in_specs=[pl.BlockSpec(memory_space=pltpu.HBM)] * 8,
        out_specs=pl.BlockSpec(memory_space=pltpu.VMEM),
        scratch_shapes=[
            pltpu.VMEM((steps, rows), bf16),
            pltpu.VMEM((HALVES, rows, half), bf16),
            pltpu.VMEM((half, modes), bf16),
            pltpu.VMEM((reduced, stress), bf16),
            pltpu.VMEM(mode_decay.shape, f32),
            pltpu.VMEM(mode_phase.shape, f32),
            pltpu.SMEM((1, 1), jnp.int32),
            pltpu.SMEM(slot_harmonic.shape, jnp.int32),
            pltpu.VMEM((steps, half), bf16),
            pltpu.VMEM((steps, half), bf16),
            pltpu.VMEM((parts, groups, ROWS, width), bf16),
            pltpu.VMEM((sectors, parts, ROWS, width), bf16),
            pltpu.VMEM((sectors, ROWS, width), bf16),
            pltpu.VMEM((groups, ROWS, half), bf16),
            pltpu.VMEM((steps, modes), f32),
            pltpu.VMEM((steps, modes), f32),
            pltpu.VMEM((groups, ROWS, width), bf16),
            pltpu.VMEM((sectors, ROWS, width), bf16),
            pltpu.VMEM((sectors, ROWS, width), bf16),
            pltpu.VMEM((groups, ROWS, half), bf16),
            pltpu.VMEM((groups, ROWS, half), bf16),
            pltpu.VMEM((2, wide, wide), bf16),
            pltpu.VMEM((2, wide, wide), bf16),
            pltpu.VMEM((8, modes), f32),
            pltpu.VMEM((8, modes), f32),
            pltpu.SemaphoreType.DMA((7 + HALVES * CHUNKS,)),
            pltpu.SemaphoreType.DMA((7,)),
            pltpu.SemaphoreType.DMA((7,)),
        ],
        compiler_params=pltpu.CompilerParams(
            collective_id=0, has_side_effects=True, vmem_limit_bytes=60 * 1024 * 1024
        ),
        cost_estimate=pl.CostEstimate(
            flops=flops, bytes_accessed=2 * reduced * (rows + stress), transcendentals=0
        ),
    )(
        load_history,
        sector_basis,
        harmonic_modes,
        stress_basis,
        mode_decay,
        mode_phase,
        mode_count.reshape(1, 1),
        slot_harmonic,
    )


def solution(mesh):
    return jax.shard_map(
        functools.partial(local, mesh.shape["sector"], mesh.shape["dof"]),
        mesh=mesh,
        in_specs=(
            P("sector", None, "dof"),
            P("dof", None),
            P("sector", None, None),
            P(None, "dof"),
            P("sector", None),
            P("sector", None),
            P("sector"),
            P(),
        ),
        out_specs=P("sector", None, "dof"),
        check_vma=False,
    )
```

```python
import functools
import math

import jax
import jax.numpy as jnp
from jax import lax
from jax.experimental import pallas as pl
from jax.experimental.pallas import tpu as pltpu
from jax.sharding import PartitionSpec as P

MESH = pl.DeviceIdType.MESH
ROWS = 16
HALVES = 2
CHUNKS = 3


def each(count, body):
    if count <= 32:
        for index in range(count):
            body(index)
    else:

        @pl.loop(0, count)
        def _(index):
            body(index)


def farthest_first(index, count, own):
    return jnp.where(own < count // 2, count - 1 - index, index)


def kernel(
    sectors,
    dofs,
    load_hbm,
    basis_hbm,
    modes_hbm,
    stress_hbm,
    decay_hbm,
    phase_hbm,
    count_hbm,
    slot_hbm,
    out_ref,
    load_v,
    basis_v,
    modes_v,
    stress_v,
    decay_v,
    phase_v,
    count_s,
    slot_s,
    pair_send,
    pair_recv,
    part_send,
    part_recv,
    spec_send,
    spec_recv,
    modal_send,
    modal_recv,
    ret_send,
    ret_recv,
    back_send,
    back_recv,
    back_other,
    fwd_table,
    bwd_table,
    power_real,
    power_imag,
    local_sem,
    send_sem,
    recv_sem,
):
    steps, reduced = load_v.shape[0], stress_v.shape[0]
    width = reduced // dofs
    half = reduced // HALVES
    groups = steps // ROWS
    parts = dofs // HALVES
    spacing = sectors // (groups * HALVES)
    mixers = groups * parts
    peers = sectors * parts
    f32, bf16 = jnp.float32, jnp.bfloat16

    own_sector = lax.axis_index("sector")
    own_dof = lax.axis_index("dof")
    own_half = lax.rem(own_dof, HALVES)
    other_half = 1 - own_half
    own_pair = own_dof // HALVES
    me = own_sector * parts + own_pair
    own_place = own_sector // spacing
    own_group = own_place // HALVES
    is_mixer = (lax.rem(own_sector, spacing) == 0) & (lax.rem(own_place, HALVES) == own_half)
    sibling = (own_sector, own_pair * HALVES + other_half)

    def device(index):
        return (index // parts, lax.rem(index, parts) * HALVES + own_half)

    def mixer_of(group, part):
        return (group * HALVES + own_half) * spacing * parts + part

    def load(src, dst, index):
        copy = pltpu.make_async_copy(src, dst, local_sem.at[index])
        copy.start()
        return copy

    def columns_of(which):
        return pl.ds(pl.multiple_of(which * half, 128), half)

    slot_copy = load(slot_hbm, slot_s, 1)
    count_copy = load(count_hbm, count_s, 2)
    decay_copy = load(decay_hbm, decay_v, 3)
    phase_copy = load(phase_hbm, phase_v, 4)
    load_copy = load(load_hbm.at[0], load_v, 0)
    chunk = load_v.shape[1] // CHUNKS
    basis_copies = [
        [
            load(
                basis_hbm.at[pl.ds(index * chunk, chunk), columns_of(which)],
                basis_v.at[turn, pl.ds(index * chunk, chunk)],
                7 + turn * CHUNKS + index,
            )
            for index in range(CHUNKS)
        ]
        for turn, which in enumerate((other_half, own_half))
    ]

    def partial_product(turn):
        total = None
        for index in range(CHUNKS):
            rows = pl.ds(index * chunk, chunk)
            basis_copies[turn][index].wait()
            term = jnp.dot(load_v[:, rows], basis_v[turn, rows, :], preferred_element_type=f32)
            total = term if total is None else total + term
        return total

    barrier = pltpu.get_barrier_semaphore()

    def greet(target):
        pl.semaphore_signal(barrier, inc=1, device_id=target, device_id_type=MESH)

    greet(sibling)

    @pl.when(is_mixer)
    def _():
        each(peers - 1, lambda index: greet(device(lax.rem(me + index + 1, peers))))

    @pl.when(jnp.logical_not(is_mixer))
    def _():
        each(mixers, lambda index: greet(device(mixer_of(index // parts, index % parts))))

    def remote(src, dst, index, target):
        return pltpu.make_async_remote_copy(
            src_ref=src,
            dst_ref=dst,
            send_sem=send_sem.at[index],
            recv_sem=recv_sem.at[index],
            device_id=target,
            device_id_type=MESH,
        )

    def send_to(src, dst, index, target):
        @pl.when(target != me)
        def _():
            remote(src, dst, index, device(target)).start()

        @pl.when(target == me)
        def _():
            pltpu.make_async_copy(src, dst, recv_sem.at[index]).start()

    def arrived(ref, index):
        pltpu.make_async_copy(ref, ref, recv_sem.at[index]).wait()

    slot_copy.wait()
    count_copy.wait()
    decay_copy.wait()
    phase_copy.wait()

    @pl.when(is_mixer)
    def _():
        wide = sectors * ROWS
        row = lax.broadcasted_iota(jnp.int32, (sectors, wide), 0)
        sector = (lax.broadcasted_iota(jnp.int32, (sectors, wide), 1) >> (ROWS.bit_length() - 1)).astype(f32)
        harmonic = jnp.zeros((sectors, wide), f32)
        for slot in range(sectors):
            harmonic = jnp.where(row == slot, slot_s[slot].astype(f32), harmonic)
        middle = float(sectors // 2)
        sine = harmonic > middle
        order = jnp.where(sine, harmonic - middle, harmonic)
        turns = order * sector
        residue = turns - float(sectors) * jnp.floor(turns * (1.0 / sectors))
        angle = residue * jnp.float32(2.0 * math.pi / sectors)
        wave = jnp.cos(angle - jnp.where(sine, jnp.float32(0.5 * math.pi), jnp.float32(0.0)))
        single = (harmonic == 0.0) | (harmonic == middle)
        weight = jnp.where(
            single, jnp.float32(math.sqrt(1.0 / sectors)), jnp.float32(math.sqrt(2.0 / sectors))
        )
        small = weight * wave
        table = jnp.broadcast_to(small[:, None, :], (sectors, ROWS, wide)).reshape(wide, wide)
        left = lax.broadcasted_iota(jnp.int32, (wide, wide), 0) & (ROWS - 1)
        right = lax.broadcasted_iota(jnp.int32, (wide, wide), 1) & (ROWS - 1)
        table = jnp.where(left == right, table, 0.0)
        for where_to, values in ((fwd_table, table), (bwd_table, table.T)):
            high = values.astype(bf16)
            where_to[0] = high
            where_to[1] = (values - high.astype(f32)).astype(bf16)

    decay = decay_v[...]
    gain = jnp.sqrt(1.0 - jnp.exp(-2.0 * decay))
    power = lax.shift_left(1, lax.broadcasted_iota(jnp.int32, power_real.shape, 0)).astype(f32)
    damping = jnp.exp(-decay * power)
    power_real[...] = damping * jnp.cos(phase_v[...] * power)
    power_imag[...] = damping * jnp.sin(phase_v[...] * power)

    load_copy.wait()
    pair_send[...] = partial_product(0).astype(bf16)

    @pl.when(is_mixer)
    def _():
        pl.semaphore_wait(barrier, peers)

    @pl.when(jnp.logical_not(is_mixer))
    def _():
        pl.semaphore_wait(barrier, mixers + 1)

    pair_copy = remote(pair_send, pair_recv, 0, sibling)
    pair_copy.start()
    product = partial_product(1)
    modes_copy = load(modes_hbm.at[0, columns_of(own_half), :], modes_v, 5)
    stress_copy = load(stress_hbm, stress_v, 6)
    pair_copy.wait_recv()
    summed = (product + pair_recv[...].astype(f32)).astype(bf16)
    for part in range(parts):
        part_send[part] = summed[:, part * width : (part + 1) * width].reshape(
            groups, ROWS, width
        )
    for turn in range(groups):
        group = farthest_first(turn, groups, own_group)
        for part in range(parts):
            send_to(
                part_send.at[part, group],
                part_recv.at[own_sector, own_pair],
                1,
                mixer_of(group, part),
            )

    def mix(table_ref, values):
        return (
            jnp.dot(table_ref[0], values, preferred_element_type=f32)
            + jnp.dot(table_ref[1], values, preferred_element_type=f32)
        ).astype(bf16)

    def spread(source, sink, which):
        dst = sink.at[own_group, :, pl.ds(pl.multiple_of(own_pair * width, 128), width)]

        def send(index):
            sector = farthest_first(index // parts, sectors, own_sector)
            target = sector * parts + index % parts
            send_to(source.at[sector], dst, which, target)

        each(peers, send)

    @pl.when(is_mixer)
    def _():
        arrived(part_recv, 1)
        total = part_recv[:, 0].astype(f32)
        for pair in range(1, parts):
            total = total + part_recv[:, pair].astype(f32)
        values = total.reshape(sectors * ROWS, width).astype(bf16)
        spec_send[...] = mix(fwd_table, values).reshape(sectors, ROWS, width)
        spread(spec_send, spec_recv, 2)

    modes_copy.wait()
    arrived(spec_recv, 2)
    modal_send[...] = jnp.dot(
        spec_recv[...].reshape(steps, half), modes_v[...], preferred_element_type=f32
    )
    modal_copy = remote(modal_send, modal_recv, 3, sibling)
    modal_copy.start()
    modal_copy.wait_recv()
    modal = modal_send[...] + modal_recv[...]
    mode = lax.broadcasted_iota(jnp.int32, modal.shape, 1)
    real = jnp.where(mode < count_s[0, 0], modal, 0.0)
    imag = None
    step = lax.broadcasted_iota(jnp.int32, modal.shape, 0)

    def later(values, lag):
        if lag % 8 == 0:
            zeros = jnp.zeros((lag, values.shape[1]), f32)
            return jnp.concatenate([zeros, values[: steps - lag]], axis=0)
        return jnp.where(step >= lag, pltpu.roll(values, lag, 0), 0.0)

    for index in range((steps - 1).bit_length()):
        turn_real, turn_imag = power_real[pl.ds(index, 1), :], power_imag[pl.ds(index, 1), :]
        old_real = later(real, 1 << index)
        if imag is None:
            imag = turn_imag * old_real
            real = real + turn_real * old_real
        else:
            old_imag = later(imag, 1 << index)
            real = real + turn_real * old_real - turn_imag * old_imag
            imag = imag + turn_real * old_imag + turn_imag * old_real
    response = (gain * real).astype(bf16)
    own_rows = modes_v[pl.ds(pl.multiple_of(own_pair * width, 128), width), :]
    returned = lax.dot_general(
        response, own_rows, (((1,), (1,)), ((), ())), preferred_element_type=f32
    )
    ret_send[...] = returned.astype(bf16).reshape(groups, ROWS, width)
    for turn in range(groups):
        group = farthest_first(turn, groups, own_group)
        send_to(ret_send.at[group], ret_recv.at[own_sector], 4, mixer_of(group, own_pair))

    @pl.when(is_mixer)
    def _():
        arrived(ret_recv, 4)
        values = ret_recv[...].reshape(sectors * ROWS, width)
        back_send[...] = mix(bwd_table, values).reshape(sectors, ROWS, width)
        spread(back_send, back_recv, 5)

    stress_copy.wait()
    arrived(back_recv, 5)
    back_copy = remote(back_recv, back_other, 6, sibling)
    back_copy.start()

    def rows_of(which):
        return stress_v[pl.ds(pl.multiple_of(which * half, 128), half), :]

    field = jnp.dot(
        back_recv[...].reshape(steps, half), rows_of(own_half), preferred_element_type=f32
    )
    back_copy.wait_recv()
    field = field + jnp.dot(
        back_other[...].reshape(steps, half), rows_of(other_half), preferred_element_type=f32
    )
    out_ref[0] = field.astype(bf16)

    def sent(ref, index):
        pltpu.make_async_copy(ref, ref, send_sem.at[index]).wait()

    pair_copy.wait_send()
    modal_copy.wait_send()
    back_copy.wait_send()

    @pl.when(is_mixer)
    def _():
        for part in range(parts):
            sent(part_send.at[part, pl.ds(0, groups - (part == 0))], 1)
        for index in (2, 5):
            sent(part_recv.at[pl.ds(0, sectors - 1)], index)
            if parts > 1:
                sent(part_recv.at[0, pl.ds(0, parts - 1)], index)
        sent(ret_send.at[pl.ds(0, groups - 1)], 4)

    @pl.when(jnp.logical_not(is_mixer))
    def _():
        sent(part_send, 1)
        sent(ret_send, 4)


def local(
    sectors,
    dofs,
    load_history,
    sector_basis,
    harmonic_modes,
    stress_basis,
    mode_decay,
    mode_phase,
    mode_count,
    slot_harmonic,
):
    _, steps, rows = load_history.shape
    reduced = sector_basis.shape[1]
    modes = harmonic_modes.shape[2]
    stress = stress_basis.shape[1]
    width = reduced // dofs
    groups = steps // ROWS
    parts = dofs // HALVES
    half = reduced // HALVES
    wide = sectors * ROWS
    bf16, f32 = jnp.bfloat16, jnp.float32
    flops = 2 * steps * reduced * (rows + stress + 2 * modes)
    return pl.pallas_call(
        functools.partial(kernel, sectors, dofs),
        out_shape=jax.ShapeDtypeStruct((1, steps, stress), bf16),
        in_specs=[pl.BlockSpec(memory_space=pltpu.HBM)] * 8,
        out_specs=pl.BlockSpec(memory_space=pltpu.VMEM),
        scratch_shapes=[
            pltpu.VMEM((steps, rows), bf16),
            pltpu.VMEM((HALVES, rows, half), bf16),
            pltpu.VMEM((half, modes), bf16),
            pltpu.VMEM((reduced, stress), bf16),
            pltpu.VMEM(mode_decay.shape, f32),
            pltpu.VMEM(mode_phase.shape, f32),
            pltpu.SMEM((1, 1), jnp.int32),
            pltpu.SMEM(slot_harmonic.shape, jnp.int32),
            pltpu.VMEM((steps, half), bf16),
            pltpu.VMEM((steps, half), bf16),
            pltpu.VMEM((parts, groups, ROWS, width), bf16),
            pltpu.VMEM((sectors, parts, ROWS, width), bf16),
            pltpu.VMEM((sectors, ROWS, width), bf16),
            pltpu.VMEM((groups, ROWS, half), bf16),
            pltpu.VMEM((steps, modes), f32),
            pltpu.VMEM((steps, modes), f32),
            pltpu.VMEM((groups, ROWS, width), bf16),
            pltpu.VMEM((sectors, ROWS, width), bf16),
            pltpu.VMEM((sectors, ROWS, width), bf16),
            pltpu.VMEM((groups, ROWS, half), bf16),
            pltpu.VMEM((groups, ROWS, half), bf16),
            pltpu.VMEM((2, wide, wide), bf16),
            pltpu.VMEM((2, wide, wide), bf16),
            pltpu.VMEM((8, modes), f32),
            pltpu.VMEM((8, modes), f32),
            pltpu.SemaphoreType.DMA((7 + HALVES * CHUNKS,)),
            pltpu.SemaphoreType.DMA((7,)),
            pltpu.SemaphoreType.DMA((7,)),
        ],
        compiler_params=pltpu.CompilerParams(
            collective_id=0, has_side_effects=True, vmem_limit_bytes=60 * 1024 * 1024
        ),
        cost_estimate=pl.CostEstimate(
            flops=flops, bytes_accessed=2 * reduced * (rows + stress), transcendentals=0
        ),
    )(
        load_history,
        sector_basis,
        harmonic_modes,
        stress_basis,
        mode_decay,
        mode_phase,
        mode_count.reshape(1, 1),
        slot_harmonic,
    )


def solution(mesh):
    return jax.shard_map(
        functools.partial(local, mesh.shape["sector"], mesh.shape["dof"]),
        mesh=mesh,
        in_specs=(
            P("sector", None, "dof"),
            P("dof", None),
            P("sector", None, None),
            P(None, "dof"),
            P("sector", None),
            P("sector", None),
            P("sector"),
            P(),
        ),
        out_specs=P("sector", None, "dof"),
        check_vma=False,
    )
```

```python
import functools
import math

import jax
import jax.numpy as jnp
from jax import lax
from jax.experimental import pallas as pl
from jax.experimental.pallas import tpu as pltpu
from jax.sharding import PartitionSpec as P

MESH = pl.DeviceIdType.MESH
ROWS = 16
HALVES = 2
CHUNKS = 3


def each(count, body):
    if count <= 32:
        for index in range(count):
            body(index)
    else:

        @pl.loop(0, count)
        def _(index):
            body(index)


def farthest_first(index, count, own):
    return jnp.where(own < count // 2, count - 1 - index, index)


def kernel(
    sectors,
    dofs,
    load_hbm,
    basis_hbm,
    modes_hbm,
    stress_hbm,
    decay_hbm,
    phase_hbm,
    count_hbm,
    slot_hbm,
    out_ref,
    load_v,
    basis_v,
    modes_v,
    stress_v,
    decay_v,
    phase_v,
    count_s,
    slot_s,
    pair_send,
    pair_recv,
    part_send,
    part_recv,
    spec_send,
    spec_recv,
    modal_send,
    modal_recv,
    ret_send,
    ret_recv,
    back_send,
    back_recv,
    back_other,
    fwd_table,
    bwd_table,
    power_real,
    power_imag,
    local_sem,
    send_sem,
    recv_sem,
    out_v,
    out_sem,
):
    steps, reduced = load_v.shape[0], stress_v.shape[0]
    width = reduced // dofs
    half = reduced // HALVES
    groups = steps // ROWS
    parts = dofs // HALVES
    spacing = sectors // (groups * HALVES)
    mixers = groups * parts
    peers = sectors * parts
    f32, bf16 = jnp.float32, jnp.bfloat16

    own_sector = lax.axis_index("sector")
    own_dof = lax.axis_index("dof")
    own_half = lax.rem(own_dof, HALVES)
    other_half = 1 - own_half
    own_pair = own_dof // HALVES
    me = own_sector * parts + own_pair
    own_place = own_sector // spacing
    own_group = own_place // HALVES
    is_mixer = (lax.rem(own_sector, spacing) == 0) & (lax.rem(own_place, HALVES) == own_half)
    sibling = (own_sector, own_pair * HALVES + other_half)

    def device(index):
        return (index // parts, lax.rem(index, parts) * HALVES + own_half)

    def mixer_of(group, part):
        return (group * HALVES + own_half) * spacing * parts + part

    def load(src, dst, index):
        copy = pltpu.make_async_copy(src, dst, local_sem.at[index])
        copy.start()
        return copy

    def columns_of(which):
        return pl.ds(pl.multiple_of(which * half, 128), half)

    slot_copy = load(slot_hbm, slot_s, 1)
    count_copy = load(count_hbm, count_s, 2)
    decay_copy = load(decay_hbm, decay_v, 3)
    phase_copy = load(phase_hbm, phase_v, 4)
    load_copy = load(load_hbm.at[0], load_v, 0)
    chunk = load_v.shape[1] // CHUNKS
    basis_copies = [
        [
            load(
                basis_hbm.at[pl.ds(index * chunk, chunk), columns_of(which)],
                basis_v.at[turn, pl.ds(index * chunk, chunk)],
                7 + turn * CHUNKS + index,
            )
            for index in range(CHUNKS)
        ]
        for turn, which in enumerate((other_half, own_half))
    ]

    def partial_product(turn):
        total = None
        for index in range(CHUNKS):
            rows = pl.ds(index * chunk, chunk)
            basis_copies[turn][index].wait()
            term = jnp.dot(load_v[:, rows], basis_v[turn, rows, :], preferred_element_type=f32)
            total = term if total is None else total + term
        return total

    barrier = pltpu.get_barrier_semaphore()

    def greet(target):
        pl.semaphore_signal(barrier, inc=1, device_id=target, device_id_type=MESH)

    greet(sibling)

    @pl.when(is_mixer)
    def _():
        each(peers - 1, lambda index: greet(device(lax.rem(me + index + 1, peers))))

    @pl.when(jnp.logical_not(is_mixer))
    def _():
        each(mixers, lambda index: greet(device(mixer_of(index // parts, index % parts))))

    def remote(src, dst, index, target):
        return pltpu.make_async_remote_copy(
            src_ref=src,
            dst_ref=dst,
            send_sem=send_sem.at[index],
            recv_sem=recv_sem.at[index],
            device_id=target,
            device_id_type=MESH,
        )

    def send_to(src, dst, index, target):
        @pl.when(target != me)
        def _():
            remote(src, dst, index, device(target)).start()

        @pl.when(target == me)
        def _():
            pltpu.make_async_copy(src, dst, recv_sem.at[index]).start()

    def arrived(ref, index):
        pltpu.make_async_copy(ref, ref, recv_sem.at[index]).wait()

    slot_copy.wait()
    count_copy.wait()
    decay_copy.wait()
    phase_copy.wait()

    @pl.when(is_mixer)
    def _():
        wide = sectors * ROWS
        row = lax.broadcasted_iota(jnp.int32, (sectors, wide), 0)
        sector = (lax.broadcasted_iota(jnp.int32, (sectors, wide), 1) >> (ROWS.bit_length() - 1)).astype(f32)
        harmonic = jnp.zeros((sectors, wide), f32)
        for slot in range(sectors):
            harmonic = jnp.where(row == slot, slot_s[slot].astype(f32), harmonic)
        middle = float(sectors // 2)
        sine = harmonic > middle
        order = jnp.where(sine, harmonic - middle, harmonic)
        turns = order * sector
        residue = turns - float(sectors) * jnp.floor(turns * (1.0 / sectors))
        angle = residue * jnp.float32(2.0 * math.pi / sectors)
        wave = jnp.cos(angle - jnp.where(sine, jnp.float32(0.5 * math.pi), jnp.float32(0.0)))
        single = (harmonic == 0.0) | (harmonic == middle)
        weight = jnp.where(
            single, jnp.float32(math.sqrt(1.0 / sectors)), jnp.float32(math.sqrt(2.0 / sectors))
        )
        small = weight * wave
        table = jnp.broadcast_to(small[:, None, :], (sectors, ROWS, wide)).reshape(wide, wide)
        left = lax.broadcasted_iota(jnp.int32, (wide, wide), 0) & (ROWS - 1)
        right = lax.broadcasted_iota(jnp.int32, (wide, wide), 1) & (ROWS - 1)
        table = jnp.where(left == right, table, 0.0)
        for where_to, values in ((fwd_table, table), (bwd_table, table.T)):
            high = values.astype(bf16)
            where_to[0] = high
            where_to[1] = (values - high.astype(f32)).astype(bf16)

    decay = decay_v[...]
    gain = jnp.sqrt(1.0 - jnp.exp(-2.0 * decay))
    power = lax.shift_left(1, lax.broadcasted_iota(jnp.int32, power_real.shape, 0)).astype(f32)
    damping = jnp.exp(-decay * power)
    power_real[...] = damping * jnp.cos(phase_v[...] * power)
    power_imag[...] = damping * jnp.sin(phase_v[...] * power)

    load_copy.wait()
    pair_send[...] = partial_product(0).astype(bf16)

    @pl.when(is_mixer)
    def _():
        pl.semaphore_wait(barrier, peers)

    @pl.when(jnp.logical_not(is_mixer))
    def _():
        pl.semaphore_wait(barrier, mixers + 1)

    pair_copy = remote(pair_send, pair_recv, 0, sibling)
    pair_copy.start()
    product = partial_product(1)
    modes_copy = load(modes_hbm.at[0, columns_of(own_half), :], modes_v, 5)
    stress_copy = load(stress_hbm, stress_v, 6)
    pair_copy.wait_recv()
    summed = (product + pair_recv[...].astype(f32)).astype(bf16)
    for part in range(parts):
        part_send[part] = summed[:, part * width : (part + 1) * width].reshape(
            groups, ROWS, width
        )
    for turn in range(groups):
        group = farthest_first(turn, groups, own_group)
        for part in range(parts):
            send_to(
                part_send.at[part, group],
                part_recv.at[own_sector, own_pair],
                1,
                mixer_of(group, part),
            )

    def mix(table_ref, values):
        return (
            jnp.dot(table_ref[0], values, preferred_element_type=f32)
            + jnp.dot(table_ref[1], values, preferred_element_type=f32)
        ).astype(bf16)

    def spread(source, sink, which):
        dst = sink.at[own_group, :, pl.ds(pl.multiple_of(own_pair * width, 128), width)]

        def send(index):
            sector = farthest_first(index // parts, sectors, own_sector)
            target = sector * parts + index % parts
            send_to(source.at[sector], dst, which, target)

        each(peers, send)

    @pl.when(is_mixer)
    def _():
        arrived(part_recv, 1)
        total = part_recv[:, 0].astype(f32)
        for pair in range(1, parts):
            total = total + part_recv[:, pair].astype(f32)
        values = total.reshape(sectors * ROWS, width).astype(bf16)
        spec_send[...] = mix(fwd_table, values).reshape(sectors, ROWS, width)
        spread(spec_send, spec_recv, 2)

    modes_copy.wait()
    arrived(spec_recv, 2)
    modal_send[...] = jnp.dot(
        spec_recv[...].reshape(steps, half), modes_v[...], preferred_element_type=f32
    )
    modal_copy = remote(modal_send, modal_recv, 3, sibling)
    modal_copy.start()
    modal_copy.wait_recv()
    modal = modal_send[...] + modal_recv[...]
    mode = lax.broadcasted_iota(jnp.int32, modal.shape, 1)
    real = jnp.where(mode < count_s[0, 0], modal, 0.0)
    imag = None
    step = lax.broadcasted_iota(jnp.int32, modal.shape, 0)

    def later(values, lag):
        if lag % 8 == 0:
            zeros = jnp.zeros((lag, values.shape[1]), f32)
            return jnp.concatenate([zeros, values[: steps - lag]], axis=0)
        return jnp.where(step >= lag, pltpu.roll(values, lag, 0), 0.0)

    for index in range((steps - 1).bit_length()):
        turn_real, turn_imag = power_real[pl.ds(index, 1), :], power_imag[pl.ds(index, 1), :]
        old_real = later(real, 1 << index)
        if imag is None:
            imag = turn_imag * old_real
            real = real + turn_real * old_real
        else:
            old_imag = later(imag, 1 << index)
            real = real + turn_real * old_real - turn_imag * old_imag
            imag = imag + turn_real * old_imag + turn_imag * old_real
    response = (gain * real).astype(bf16)
    own_rows = modes_v[pl.ds(pl.multiple_of(own_pair * width, 128), width), :]
    returned = lax.dot_general(
        response, own_rows, (((1,), (1,)), ((), ())), preferred_element_type=f32
    )
    ret_send[...] = returned.astype(bf16).reshape(groups, ROWS, width)
    for turn in range(groups):
        group = farthest_first(turn, groups, own_group)
        send_to(ret_send.at[group], ret_recv.at[own_sector], 4, mixer_of(group, own_pair))

    @pl.when(is_mixer)
    def _():
        arrived(ret_recv, 4)
        values = ret_recv[...].reshape(sectors * ROWS, width)
        back_send[...] = mix(bwd_table, values).reshape(sectors, ROWS, width)
        spread(back_send, back_recv, 5)

    stress_copy.wait()
    arrived(back_recv, 5)
    back_copy = remote(back_recv, back_other, 6, sibling)
    back_copy.start()

    piece = out_v.shape[1] // CHUNKS

    def product_of(ref, which, index):
        rows = pl.ds(pl.multiple_of(which * half, 128), half)
        return jnp.dot(
            ref[...].reshape(steps, half),
            stress_v[rows, index * piece : (index + 1) * piece],
            preferred_element_type=f32,
        )

    fields = [product_of(back_recv, own_half, index) for index in range(CHUNKS)]
    back_copy.wait_recv()
    out_copies = []
    for index in range(CHUNKS):
        columns = pl.ds(index * piece, piece)
        field = fields[index] + product_of(back_other, other_half, index)
        out_v[:, columns] = field.astype(bf16)
        copy = pltpu.make_async_copy(
            out_v.at[:, columns], out_ref.at[0, :, columns], out_sem.at[index]
        )
        copy.start()
        out_copies.append(copy)

    def sent(ref, index):
        pltpu.make_async_copy(ref, ref, send_sem.at[index]).wait()

    for copy in out_copies:
        copy.wait()
    pair_copy.wait_send()
    modal_copy.wait_send()
    back_copy.wait_send()

    @pl.when(is_mixer)
    def _():
        for part in range(parts):
            sent(part_send.at[part, pl.ds(0, groups - (part == 0))], 1)
        for index in (2, 5):
            sent(part_recv.at[pl.ds(0, sectors - 1)], index)
            if parts > 1:
                sent(part_recv.at[0, pl.ds(0, parts - 1)], index)
        sent(ret_send.at[pl.ds(0, groups - 1)], 4)

    @pl.when(jnp.logical_not(is_mixer))
    def _():
        sent(part_send, 1)
        sent(ret_send, 4)


def local(
    sectors,
    dofs,
    load_history,
    sector_basis,
    harmonic_modes,
    stress_basis,
    mode_decay,
    mode_phase,
    mode_count,
    slot_harmonic,
):
    _, steps, rows = load_history.shape
    reduced = sector_basis.shape[1]
    modes = harmonic_modes.shape[2]
    stress = stress_basis.shape[1]
    width = reduced // dofs
    groups = steps // ROWS
    parts = dofs // HALVES
    half = reduced // HALVES
    wide = sectors * ROWS
    bf16, f32 = jnp.bfloat16, jnp.float32
    flops = 2 * steps * reduced * (rows + stress + 2 * modes)
    return pl.pallas_call(
        functools.partial(kernel, sectors, dofs),
        out_shape=jax.ShapeDtypeStruct((1, steps, stress), bf16),
        in_specs=[pl.BlockSpec(memory_space=pltpu.HBM)] * 8,
        out_specs=pl.BlockSpec(memory_space=pl.ANY),
        scratch_shapes=[
            pltpu.VMEM((steps, rows), bf16),
            pltpu.VMEM((HALVES, rows, half), bf16),
            pltpu.VMEM((half, modes), bf16),
            pltpu.VMEM((reduced, stress), bf16),
            pltpu.VMEM(mode_decay.shape, f32),
            pltpu.VMEM(mode_phase.shape, f32),
            pltpu.SMEM((1, 1), jnp.int32),
            pltpu.SMEM(slot_harmonic.shape, jnp.int32),
            pltpu.VMEM((steps, half), bf16),
            pltpu.VMEM((steps, half), bf16),
            pltpu.VMEM((parts, groups, ROWS, width), bf16),
            pltpu.VMEM((sectors, parts, ROWS, width), bf16),
            pltpu.VMEM((sectors, ROWS, width), bf16),
            pltpu.VMEM((groups, ROWS, half), bf16),
            pltpu.VMEM((steps, modes), f32),
            pltpu.VMEM((steps, modes), f32),
            pltpu.VMEM((groups, ROWS, width), bf16),
            pltpu.VMEM((sectors, ROWS, width), bf16),
            pltpu.VMEM((sectors, ROWS, width), bf16),
            pltpu.VMEM((groups, ROWS, half), bf16),
            pltpu.VMEM((groups, ROWS, half), bf16),
            pltpu.VMEM((2, wide, wide), bf16),
            pltpu.VMEM((2, wide, wide), bf16),
            pltpu.VMEM((8, modes), f32),
            pltpu.VMEM((8, modes), f32),
            pltpu.SemaphoreType.DMA((7 + HALVES * CHUNKS,)),
            pltpu.SemaphoreType.DMA((7,)),
            pltpu.SemaphoreType.DMA((7,)),
            pltpu.VMEM((steps, stress), bf16),
            pltpu.SemaphoreType.DMA((CHUNKS,)),
        ],
        compiler_params=pltpu.CompilerParams(
            collective_id=0, has_side_effects=True, vmem_limit_bytes=60 * 1024 * 1024
        ),
        cost_estimate=pl.CostEstimate(
            flops=flops, bytes_accessed=2 * reduced * (rows + stress), transcendentals=0
        ),
    )(
        load_history,
        sector_basis,
        harmonic_modes,
        stress_basis,
        mode_decay,
        mode_phase,
        mode_count.reshape(1, 1),
        slot_harmonic,
    )


def solution(mesh):
    return jax.shard_map(
        functools.partial(local, mesh.shape["sector"], mesh.shape["dof"]),
        mesh=mesh,
        in_specs=(
            P("sector", None, "dof"),
            P("dof", None),
            P("sector", None, None),
            P(None, "dof"),
            P("sector", None),
            P("sector", None),
            P("sector"),
            P(),
        ),
        out_specs=P("sector", None, "dof"),
        check_vma=False,
    )
```

```python
import functools
import math

import jax
import jax.numpy as jnp
from jax import lax
from jax.experimental import pallas as pl
from jax.experimental.pallas import tpu as pltpu
from jax.sharding import PartitionSpec as P

MESH = pl.DeviceIdType.MESH
ROWS = 16
HALVES = 2
CHUNKS = 3


def each(count, body):
    if count <= 32:
        for index in range(count):
            body(index)
    else:

        @pl.loop(0, count)
        def _(index):
            body(index)


def farthest_first(index, count, own):
    return jnp.where(own < count // 2, count - 1 - index, index)


def kernel(
    sectors,
    dofs,
    load_hbm,
    basis_hbm,
    modes_hbm,
    stress_hbm,
    decay_hbm,
    phase_hbm,
    count_hbm,
    slot_hbm,
    out_ref,
    load_v,
    basis_v,
    modes_v,
    stress_v,
    decay_v,
    phase_v,
    count_s,
    slot_s,
    pair_send,
    pair_recv,
    part_send,
    part_recv,
    spec_send,
    spec_recv,
    modal_send,
    modal_recv,
    ret_send,
    ret_recv,
    back_send,
    back_recv,
    back_other,
    fwd_table,
    bwd_table,
    power_real,
    power_imag,
    local_sem,
    send_sem,
    recv_sem,
    out_v,
    out_sem,
):
    steps, reduced = load_v.shape[0], stress_v.shape[0]
    width = reduced // dofs
    half = reduced // HALVES
    groups = steps // ROWS
    parts = dofs // HALVES
    spacing = sectors // (groups * HALVES)
    mixers = groups * parts
    peers = sectors * parts
    f32, bf16 = jnp.float32, jnp.bfloat16

    own_sector = lax.axis_index("sector")
    own_dof = lax.axis_index("dof")
    own_half = lax.rem(own_dof, HALVES)
    other_half = 1 - own_half
    own_pair = own_dof // HALVES
    me = own_sector * parts + own_pair
    own_place = own_sector // spacing
    own_group = own_place // HALVES
    is_mixer = (lax.rem(own_sector, spacing) == 0) & (lax.rem(own_place, HALVES) == own_half)
    sibling = (own_sector, own_pair * HALVES + other_half)

    def device(index):
        return (index // parts, lax.rem(index, parts) * HALVES + own_half)

    def mixer_of(group, part):
        return (group * HALVES + own_half) * spacing * parts + part

    def load(src, dst, index):
        copy = pltpu.make_async_copy(src, dst, local_sem.at[index])
        copy.start()
        return copy

    def columns_of(which):
        return pl.ds(pl.multiple_of(which * half, 128), half)

    slot_copy = load(slot_hbm, slot_s, 1)
    count_copy = load(count_hbm, count_s, 2)
    decay_copy = load(decay_hbm, decay_v, 3)
    phase_copy = load(phase_hbm, phase_v, 4)
    load_copy = load(load_hbm.at[0], load_v, 0)
    chunk = load_v.shape[1] // CHUNKS
    basis_copies = [
        [
            load(
                basis_hbm.at[pl.ds(index * chunk, chunk), columns_of(which)],
                basis_v.at[turn, pl.ds(index * chunk, chunk)],
                7 + turn * CHUNKS + index,
            )
            for index in range(CHUNKS)
        ]
        for turn, which in enumerate((other_half, own_half))
    ]

    def partial_product(turn):
        total = None
        for index in range(CHUNKS):
            rows = pl.ds(index * chunk, chunk)
            basis_copies[turn][index].wait()
            term = jnp.dot(load_v[:, rows], basis_v[turn, rows, :], preferred_element_type=f32)
            total = term if total is None else total + term
        return total

    barrier = pltpu.get_barrier_semaphore()

    def greet(target):
        pl.semaphore_signal(barrier, inc=1, device_id=target, device_id_type=MESH)

    greet(sibling)

    @pl.when(is_mixer)
    def _():
        each(peers - 1, lambda index: greet(device(lax.rem(me + index + 1, peers))))

    @pl.when(jnp.logical_not(is_mixer))
    def _():
        each(mixers, lambda index: greet(device(mixer_of(index // parts, index % parts))))

    def remote(src, dst, index, target):
        return pltpu.make_async_remote_copy(
            src_ref=src,
            dst_ref=dst,
            send_sem=send_sem.at[index],
            recv_sem=recv_sem.at[index],
            device_id=target,
            device_id_type=MESH,
        )

    def send_to(src, dst, index, target):
        @pl.when(target != me)
        def _():
            remote(src, dst, index, device(target)).start()

        @pl.when(target == me)
        def _():
            pltpu.make_async_copy(src, dst, recv_sem.at[index]).start()

    def arrived(ref, index):
        pltpu.make_async_copy(ref, ref, recv_sem.at[index]).wait()

    slot_copy.wait()
    count_copy.wait()
    decay_copy.wait()
    phase_copy.wait()

    @pl.when(is_mixer)
    def _():
        wide = sectors * ROWS
        row = lax.broadcasted_iota(jnp.int32, (sectors, wide), 0)
        sector = (lax.broadcasted_iota(jnp.int32, (sectors, wide), 1) >> (ROWS.bit_length() - 1)).astype(f32)
        harmonic = jnp.zeros((sectors, wide), f32)
        for slot in range(sectors):
            harmonic = jnp.where(row == slot, slot_s[slot].astype(f32), harmonic)
        middle = float(sectors // 2)
        sine = harmonic > middle
        order = jnp.where(sine, harmonic - middle, harmonic)
        turns = order * sector
        residue = turns - float(sectors) * jnp.floor(turns * (1.0 / sectors))
        angle = residue * jnp.float32(2.0 * math.pi / sectors)
        wave = jnp.cos(angle - jnp.where(sine, jnp.float32(0.5 * math.pi), jnp.float32(0.0)))
        single = (harmonic == 0.0) | (harmonic == middle)
        weight = jnp.where(
            single, jnp.float32(math.sqrt(1.0 / sectors)), jnp.float32(math.sqrt(2.0 / sectors))
        )
        small = weight * wave
        table = jnp.broadcast_to(small[:, None, :], (sectors, ROWS, wide)).reshape(wide, wide)
        left = lax.broadcasted_iota(jnp.int32, (wide, wide), 0) & (ROWS - 1)
        right = lax.broadcasted_iota(jnp.int32, (wide, wide), 1) & (ROWS - 1)
        table = jnp.where(left == right, table, 0.0)
        for where_to, values in ((fwd_table, table), (bwd_table, table.T)):
            high = values.astype(bf16)
            where_to[0] = high
            where_to[1] = (values - high.astype(f32)).astype(bf16)

    decay = decay_v[...]
    gain = jnp.sqrt(1.0 - jnp.exp(-2.0 * decay))
    power = lax.shift_left(1, lax.broadcasted_iota(jnp.int32, power_real.shape, 0)).astype(f32)
    damping = jnp.exp(-decay * power)
    power_real[...] = damping * jnp.cos(phase_v[...] * power)
    power_imag[...] = damping * jnp.sin(phase_v[...] * power)

    load_copy.wait()
    pair_send[...] = partial_product(0).astype(bf16)

    @pl.when(is_mixer)
    def _():
        pl.semaphore_wait(barrier, peers)

    @pl.when(jnp.logical_not(is_mixer))
    def _():
        pl.semaphore_wait(barrier, mixers + 1)

    pair_copy = remote(pair_send, pair_recv, 0, sibling)
    pair_copy.start()
    for copy in basis_copies[1]:
        copy.wait()
    product = jnp.dot(load_v[...], basis_v[1], preferred_element_type=f32)
    modes_copy = load(modes_hbm.at[0, columns_of(own_half), :], modes_v, 5)
    stress_copy = load(stress_hbm, stress_v, 6)
    pair_copy.wait_recv()
    for part in range(parts):
        columns = slice(part * width, (part + 1) * width)
        summed = (product[:, columns] + pair_recv[:, columns].astype(f32)).astype(bf16)
        part_send[part] = summed.reshape(groups, ROWS, width)
        for turn in range(groups):
            group = farthest_first(turn, groups, own_group)
            send_to(
                part_send.at[part, group],
                part_recv.at[own_sector, own_pair],
                1,
                mixer_of(group, part),
            )

    def mix(table_ref, values):
        return (
            jnp.dot(table_ref[0], values, preferred_element_type=f32)
            + jnp.dot(table_ref[1], values, preferred_element_type=f32)
        ).astype(bf16)

    def spread(source, sink, which):
        dst = sink.at[own_group, :, pl.ds(pl.multiple_of(own_pair * width, 128), width)]

        def send(index):
            sector = farthest_first(index // parts, sectors, own_sector)
            target = sector * parts + index % parts
            send_to(source.at[sector], dst, which, target)

        each(peers, send)

    @pl.when(is_mixer)
    def _():
        arrived(part_recv, 1)
        total = part_recv[:, 0].astype(f32)
        for pair in range(1, parts):
            total = total + part_recv[:, pair].astype(f32)
        values = total.reshape(sectors * ROWS, width).astype(bf16)
        spec_send[...] = mix(fwd_table, values).reshape(sectors, ROWS, width)
        spread(spec_send, spec_recv, 2)

    modes_copy.wait()
    arrived(spec_recv, 2)
    modal_send[...] = jnp.dot(
        spec_recv[...].reshape(steps, half), modes_v[...], preferred_element_type=f32
    )
    modal_copy = remote(modal_send, modal_recv, 3, sibling)
    modal_copy.start()
    modal_copy.wait_recv()
    modal = modal_send[...] + modal_recv[...]
    mode = lax.broadcasted_iota(jnp.int32, modal.shape, 1)
    real = jnp.where(mode < count_s[0, 0], modal, 0.0)
    imag = None
    step = lax.broadcasted_iota(jnp.int32, modal.shape, 0)

    def later(values, lag):
        if lag % 8 == 0:
            zeros = jnp.zeros((lag, values.shape[1]), f32)
            return jnp.concatenate([zeros, values[: steps - lag]], axis=0)
        return jnp.where(step >= lag, pltpu.roll(values, lag, 0), 0.0)

    for index in range((steps - 1).bit_length()):
        turn_real, turn_imag = power_real[pl.ds(index, 1), :], power_imag[pl.ds(index, 1), :]
        old_real = later(real, 1 << index)
        if imag is None:
            imag = turn_imag * old_real
            real = real + turn_real * old_real
        else:
            old_imag = later(imag, 1 << index)
            real = real + turn_real * old_real - turn_imag * old_imag
            imag = imag + turn_real * old_imag + turn_imag * old_real
    response = (gain * real).astype(bf16)
    own_rows = modes_v[pl.ds(pl.multiple_of(own_pair * width, 128), width), :]
    returned = lax.dot_general(
        response, own_rows, (((1,), (1,)), ((), ())), preferred_element_type=f32
    )
    ret_send[...] = returned.astype(bf16).reshape(groups, ROWS, width)
    for turn in range(groups):
        group = farthest_first(turn, groups, own_group)
        send_to(ret_send.at[group], ret_recv.at[own_sector], 4, mixer_of(group, own_pair))

    @pl.when(is_mixer)
    def _():
        arrived(ret_recv, 4)
        values = ret_recv[...].reshape(sectors * ROWS, width)
        back_send[...] = mix(bwd_table, values).reshape(sectors, ROWS, width)
        spread(back_send, back_recv, 5)

    stress_copy.wait()
    arrived(back_recv, 5)
    back_copy = remote(back_recv, back_other, 6, sibling)
    back_copy.start()

    piece = out_v.shape[1] // CHUNKS

    def product_of(ref, which, index):
        rows = pl.ds(pl.multiple_of(which * half, 128), half)
        return jnp.dot(
            ref[...].reshape(steps, half),
            stress_v[rows, index * piece : (index + 1) * piece],
            preferred_element_type=f32,
        )

    fields = [product_of(back_recv, own_half, index) for index in range(CHUNKS)]
    back_copy.wait_recv()
    out_copies = []
    for index in range(CHUNKS):
        columns = pl.ds(index * piece, piece)
        field = fields[index] + product_of(back_other, other_half, index)
        out_v[:, columns] = field.astype(bf16)
        copy = pltpu.make_async_copy(
            out_v.at[:, columns], out_ref.at[0, :, columns], out_sem.at[index]
        )
        copy.start()
        out_copies.append(copy)

    def sent(ref, index):
        pltpu.make_async_copy(ref, ref, send_sem.at[index]).wait()

    for copy in out_copies:
        copy.wait()
    pair_copy.wait_send()
    modal_copy.wait_send()
    back_copy.wait_send()

    @pl.when(is_mixer)
    def _():
        for part in range(parts):
            sent(part_send.at[part, pl.ds(0, groups - (part == 0))], 1)
        for index in (2, 5):
            sent(part_recv.at[pl.ds(0, sectors - 1)], index)
            if parts > 1:
                sent(part_recv.at[0, pl.ds(0, parts - 1)], index)
        sent(ret_send.at[pl.ds(0, groups - 1)], 4)

    @pl.when(jnp.logical_not(is_mixer))
    def _():
        sent(part_send, 1)
        sent(ret_send, 4)


def local(
    sectors,
    dofs,
    load_history,
    sector_basis,
    harmonic_modes,
    stress_basis,
    mode_decay,
    mode_phase,
    mode_count,
    slot_harmonic,
):
    _, steps, rows = load_history.shape
    reduced = sector_basis.shape[1]
    modes = harmonic_modes.shape[2]
    stress = stress_basis.shape[1]
    width = reduced // dofs
    groups = steps // ROWS
    parts = dofs // HALVES
    half = reduced // HALVES
    wide = sectors * ROWS
    bf16, f32 = jnp.bfloat16, jnp.float32
    flops = 2 * steps * reduced * (rows + stress + 2 * modes)
    return pl.pallas_call(
        functools.partial(kernel, sectors, dofs),
        out_shape=jax.ShapeDtypeStruct((1, steps, stress), bf16),
        in_specs=[pl.BlockSpec(memory_space=pltpu.HBM)] * 8,
        out_specs=pl.BlockSpec(memory_space=pl.ANY),
        scratch_shapes=[
            pltpu.VMEM((steps, rows), bf16),
            pltpu.VMEM((HALVES, rows, half), bf16),
            pltpu.VMEM((half, modes), bf16),
            pltpu.VMEM((reduced, stress), bf16),
            pltpu.VMEM(mode_decay.shape, f32),
            pltpu.VMEM(mode_phase.shape, f32),
            pltpu.SMEM((1, 1), jnp.int32),
            pltpu.SMEM(slot_harmonic.shape, jnp.int32),
            pltpu.VMEM((steps, half), bf16),
            pltpu.VMEM((steps, half), bf16),
            pltpu.VMEM((parts, groups, ROWS, width), bf16),
            pltpu.VMEM((sectors, parts, ROWS, width), bf16),
            pltpu.VMEM((sectors, ROWS, width), bf16),
            pltpu.VMEM((groups, ROWS, half), bf16),
            pltpu.VMEM((steps, modes), f32),
            pltpu.VMEM((steps, modes), f32),
            pltpu.VMEM((groups, ROWS, width), bf16),
            pltpu.VMEM((sectors, ROWS, width), bf16),
            pltpu.VMEM((sectors, ROWS, width), bf16),
            pltpu.VMEM((groups, ROWS, half), bf16),
            pltpu.VMEM((groups, ROWS, half), bf16),
            pltpu.VMEM((2, wide, wide), bf16),
            pltpu.VMEM((2, wide, wide), bf16),
            pltpu.VMEM((8, modes), f32),
            pltpu.VMEM((8, modes), f32),
            pltpu.SemaphoreType.DMA((7 + HALVES * CHUNKS,)),
            pltpu.SemaphoreType.DMA((7,)),
            pltpu.SemaphoreType.DMA((7,)),
            pltpu.VMEM((steps, stress), bf16),
            pltpu.SemaphoreType.DMA((CHUNKS,)),
        ],
        compiler_params=pltpu.CompilerParams(
            collective_id=0, has_side_effects=True, vmem_limit_bytes=60 * 1024 * 1024
        ),
        cost_estimate=pl.CostEstimate(
            flops=flops, bytes_accessed=2 * reduced * (rows + stress), transcendentals=0
        ),
    )(
        load_history,
        sector_basis,
        harmonic_modes,
        stress_basis,
        mode_decay,
        mode_phase,
        mode_count.reshape(1, 1),
        slot_harmonic,
    )


def solution(mesh):
    return jax.shard_map(
        functools.partial(local, mesh.shape["sector"], mesh.shape["dof"]),
        mesh=mesh,
        in_specs=(
            P("sector", None, "dof"),
            P("dof", None),
            P("sector", None, None),
            P(None, "dof"),
            P("sector", None),
            P("sector", None),
            P("sector"),
            P(),
        ),
        out_specs=P("sector", None, "dof"),
        check_vma=False,
    )
```
